32 devices in a mesh: gz: 2 (over x), xy: 16 (over z, y, core).
Axes of the slice: x: 2, y: 2, z: 4, core: 2. Of those that a mesh axis runs over, the one named last changes fastest.
Arguments:
- fixed: float32 [16, 256, 1024], P('gz', 'xy'), may hold values from -6 to 6
- moving: float32 [16, 256, 1024], P('gz', 'xy'), may hold values from -9 to 9
Outputs:
- update: float32 [3, 16, 256, 1024], P(None, 'gz', 'xy')
The draws below stay inside these ranges and needn't reach their ends.
All inputs are finite; a program needn't handle non-finite values.
Results may differ from the reference program's by a relative error of at most 0.00016.
Values sent between devices are 32-bit elements; how exact they have to be, the bound alone decides.
A program may use at most 64 MiB of HBM per device.

```python
import jax
import jax.numpy as jnp
from jax import lax

RADIUS = 4
SPACING = 8
NX = 1024
NZ = 16
NY = 256


def image_pair(key):
    first_key, second_key = jax.random.split(jax.random.fold_in(key, 7))
    shape = (NZ, NY, NX)
    base = jnp.clip(jax.random.normal(first_key, shape, jnp.float32), -6.0, 6.0)
    noise = jnp.clip(jax.random.normal(second_key, shape, jnp.float32), -6.0, 6.0)
    lower, upper = (0.1, 0.8)
    plane = jnp.arange(NZ).astype(jnp.float32) / NZ
    row = jnp.arange(NY).astype(jnp.float32) / NY
    weight = lower + (upper - lower) * 0.5 * (plane[:, None, None] + row[None, :, None])
    moved = weight * base + jnp.sqrt(1.0 - weight * weight) * noise
    return (base, moved)


def draw_fixed(key, part):
    return image_pair(key)[0].astype(jnp.float32)


def draw_moving(key, part):
    return image_pair(key)[1].astype(jnp.float32)


def setup_inputs(seed: int = 0) -> dict:
    arg_keys = jax.random.split(jax.random.key(seed), 3)
    return {
        "fixed": draw_fixed(jax.random.fold_in(arg_keys[2], 71), 0),
        "moving": draw_moving(jax.random.fold_in(arg_keys[2], 71), 0),
    }


HIGH = lax.Precision.HIGHEST
EPS = 1e-05

def basis(index, knot):
    span = index // SPACING
    frac = (index - span * SPACING).astype(jnp.float32) / SPACING
    offset = knot - span
    other = 1.0 - frac
    first = other * other * other / 6.0
    second = (3.0 * frac ** 3 - 6.0 * frac ** 2 + 4.0) / 6.0
    third = (-3.0 * frac ** 3 + 3.0 * frac ** 2 + 3.0 * frac + 1.0) / 6.0
    fourth = frac ** 3 / 6.0
    zero = jnp.zeros_like(frac)
    return jnp.where(offset == 0, first, jnp.where(offset == 1, second, jnp.where(offset == 2, third, jnp.where(offset == 3, fourth, zero))))

def square_total(index):
    span = index // SPACING
    total = basis(index, span) ** 2
    for step in range(1, 4):
        total = total + basis(index, span + step) ** 2
    return total

def fit_matrix(index, knot):
    value = basis(index, knot)
    return value * value * value / square_total(index)

def knot_mass(knot, extent):
    spans = extent // SPACING
    within = jnp.arange(SPACING).astype(jnp.int32)
    offsets = jnp.arange(4).astype(jnp.int32)
    energy = lax.optimization_barrier(jnp.sum(basis(within[None, :], offsets[:, None]) ** 2, axis=1))
    start = knot[:, None] - offsets[None, :]
    valid = (start >= 0) & (start <= spans - 1)
    return lax.optimization_barrier(jnp.sum(jnp.where(valid, energy[None, :], jnp.zeros_like(energy)[None, :]), axis=1))

def window_sum(padded, shape):
    depth, rows, width = shape
    span = 2 * RADIUS + 1
    acc = padded[0:depth]
    for step in range(1, span):
        acc = acc + padded[step:step + depth]
    out = acc[:, 0:rows]
    for step in range(1, span):
        out = out + acc[:, step:step + rows]
    res = out[:, :, 0:width]
    for step in range(1, span):
        res = res + out[:, :, step:step + width]
    return res

def cc_force(fpad, mpad, shape):
    depth, rows, width = shape
    count = float((2 * RADIUS + 1) ** 3)
    sum_f = window_sum(fpad, shape)
    sum_m = window_sum(mpad, shape)
    sum_ff = window_sum(fpad * fpad, shape)
    sum_mm = window_sum(mpad * mpad, shape)
    sum_fm = window_sum(fpad * mpad, shape)
    r = RADIUS
    centre_f = fpad[r:r + depth, r:r + rows, r:r + width]
    centre_m = mpad[r:r + depth, r:r + rows, r:r + width]
    grad_z = (mpad[r + 1:r + 1 + depth, r:r + rows, r:r + width] - mpad[r - 1:r - 1 + depth, r:r + rows, r:r + width]) * 0.5
    grad_y = (mpad[r:r + depth, r + 1:r + 1 + rows, r:r + width] - mpad[r:r + depth, r - 1:r - 1 + rows, r:r + width]) * 0.5
    grad_x = (mpad[r:r + depth, r:r + rows, r + 1:r + 1 + width] - mpad[r:r + depth, r:r + rows, r - 1:r - 1 + width]) * 0.5
    mean_f = sum_f / count
    mean_m = sum_m / count
    cov = sum_fm / count - mean_f * mean_m
    var_f = sum_ff / count - mean_f * mean_f
    var_m = sum_mm / count - mean_m * mean_m
    factor = 2.0 * cov / (var_f * var_m + EPS)
    resid = centre_f - mean_f - cov / (var_m + EPS) * (centre_m - mean_m)
    common = factor * resid
    return jnp.stack([common * grad_z, common * grad_y, common * grad_x])

def reference(fixed, moving):
    depth, rows, width = fixed.shape
    fpad = jnp.pad(fixed, RADIUS)
    mpad = jnp.pad(moving, RADIUS)
    force = cc_force(fpad, mpad, (depth, rows, width))
    knots_z = depth // SPACING + 3
    knots_y = rows // SPACING + 3
    knots_x = width // SPACING + 3
    vox_z = jnp.arange(depth).astype(jnp.int32)
    vox_y = jnp.arange(rows).astype(jnp.int32)
    vox_x = jnp.arange(width).astype(jnp.int32)
    ctl_z = jnp.arange(knots_z).astype(jnp.int32)
    ctl_y = jnp.arange(knots_y).astype(jnp.int32)
    ctl_x = jnp.arange(knots_x).astype(jnp.int32)
    fit_z = fit_matrix(vox_z[None, :], ctl_z[:, None])
    fit_y = fit_matrix(vox_y[None, :], ctl_y[:, None])
    fit_x = fit_matrix(vox_x[None, :], ctl_x[:, None])
    numer = jnp.einsum('kzyx,cx->kzyc', force, fit_x, precision=HIGH)
    numer = jnp.einsum('kzyc,by->kzbc', numer, fit_y, precision=HIGH)
    numer = jnp.einsum('kzbc,az->kabc', numer, fit_z, precision=HIGH)
    mass = knot_mass(ctl_z, depth)[:, None, None] * knot_mass(ctl_y, rows)[None, :, None] * knot_mass(ctl_x, width)[None, None, :]
    coef = numer / mass[None]
    eval_z = basis(vox_z[:, None], ctl_z[None, :])
    eval_y = basis(vox_y[:, None], ctl_y[None, :])
    eval_x = basis(vox_x[:, None], ctl_x[None, :])
    field = jnp.einsum('kabc,xc->kabx', coef, eval_x, precision=HIGH)
    field = jnp.einsum('kabx,yb->kayx', field, eval_y, precision=HIGH)
    field = jnp.einsum('kayx,za->kzyx', field, eval_z, precision=HIGH)
    power = jnp.mean(field * field)
    return field / (jnp.sqrt(power) + 1e-06)
```

```python
import functools

import jax
import jax.numpy as jnp
import numpy as np
from jax import lax
from jax.experimental import pallas as pl
from jax.experimental.pallas import tpu as pltpu
from jax.sharding import PartitionSpec as P

RADIUS = 4
SPACING = 8
HIGH = lax.Precision.HIGHEST
EPS = 1e-05
MESH = pl.DeviceIdType.MESH
LANE = 128


def np_basis(index, knot):
    span = index // SPACING
    t = (index - span * SPACING) / SPACING
    j = knot - span
    values = (
        (1 - t) ** 3 / 6,
        (3 * t**3 - 6 * t**2 + 4) / 6,
        (-3 * t**3 + 3 * t**2 + 3 * t + 1) / 6,
        t**3 / 6,
    )
    out = np.zeros(np.broadcast(index, knot).shape)
    for step in range(4):
        out = np.where(j == step, values[step], out)
    return out


def np_tables(extent):
    index = np.arange(extent)[:, None]
    value = np_basis(index, np.arange(extent // SPACING + 3)[None, :])
    return value, value**3 / (value**2).sum(axis=1, keepdims=True)


def energies():
    index = np.arange(SPACING)
    return [float((np_basis(index, np.full(SPACING, j)) ** 2).sum()) for j in range(4)]


def mass_of(knot, extent):
    total = jnp.zeros(knot.shape, jnp.float32)
    for j, energy in enumerate(energies()):
        start = knot - j
        total = total + jnp.where((start >= 0) & (start <= extent // SPACING - 1), energy, 0.0)
    return total


def group_size(count):
    size = 1
    while size * size < count and count % (size * 2) == 0:
        size *= 2
    return size


def dot(a, b):
    return jnp.dot(a, b, precision=HIGH, preferred_element_type=jnp.float32)


def kernel(
    n_z, n_y, depth, rows, width, group, ctl_pad,
    fitz_ref, f_hbm, m_hbm, fitx_hbm, evalx_hbm, gram_hbm, fity_ref, evalzy_ref,
    field_ref, scale_ref,
    img, packout, packin, ysum, grady, acc, fitx, evalx, gram, part, part_z, part_y,
    power_out, power_in,
    own_sem, const_sem, zs_sem, zr_sem, ys_sem, yr_sem, fs_sem, fr_sem,
    pzs_sem, pzr_sem, pys_sem, pyr_sem, ws_sem, wr_sem,
):
    r = RADIUS
    slab, strip = lax.axis_index("gz"), lax.axis_index("xy")
    span_z, span_y = depth // SPACING, rows // SPACING
    knots_z, knots_y = span_z + 3, span_y + 3
    reach_z = min((span_z + 2) // span_z, n_z - 1)
    reach_y = min((span_y + 2) // span_y, n_y - 1)
    pad_rows = fity_ref.shape[0] // knots_y
    up, down = slab < n_z - 1, slab > 0
    right, left = strip < n_y - 1, strip > 0
    after = rows + 2 * r

    own = [
        pltpu.make_async_copy(ref, img.at[i, pl.ds(r, depth)], own_sem.at[i])
        for i, ref in enumerate((f_hbm, m_hbm))
    ]
    consts = [
        pltpu.make_async_copy(src, dst, const_sem.at[i])
        for i, (src, dst) in enumerate(((fitx_hbm, fitx), (evalx_hbm, evalx), (gram_hbm, gram)))
    ]
    for copy in own:
        copy.start()

    barrier = pltpu.get_barrier_semaphore()
    lo_block = (strip // group) * group
    here = strip % group
    groups = n_y // group

    def beside(dist):
        if dist % group == 0:
            return []
        below = (strip >= dist) & (here < dist % group)
        above = (strip < n_y - dist) & (here >= group - dist % group)
        if dist > group:
            below, above = strip >= dist, strip < n_y - dist
        return [(below, strip - dist), (above, strip + dist)]

    def inner(step):
        place = (slab * group + here + step) % (n_z * group)
        return (place // group, lo_block + place % group)

    def outer(step):
        return (slab, (strip + step * group) % n_y)

    def greet(device):
        pl.semaphore_signal(barrier, inc=1, device_id=device, device_id_type=MESH)

    heard = n_z * group - 1 + groups - 1
    for step in range(1, n_z * group):
        greet(inner(step))
    for step in range(1, groups):
        greet(outer(step))
    for dist in range(1, reach_y + 1):
        for there, other in beside(dist):
            pl.when(there)(functools.partial(greet, (slab, other)))
            heard = heard + jnp.where(there, 1, 0)
    pl.semaphore_wait(barrier, heard)

    def zcopy(side, h, i):
        ref = (f_hbm, m_hbm)[i]
        src = h if side == 0 else depth - 1 - h
        dst = depth + r + h if side == 0 else r - 1 - h
        target = slab - 1 if side == 0 else slab + 1
        return pltpu.make_async_remote_copy(
            src_ref=ref.at[src], dst_ref=img.at[i, dst],
            send_sem=zs_sem.at[side, h, i], recv_sem=zr_sem.at[1 - side, h, i],
            device_id=(target, strip), device_id_type=MESH,
        )

    def zsends(act):
        for h in range(r):
            for i in range(2):
                pl.when(up)(lambda: act(zcopy(1, h, i)))
                pl.when(down)(lambda: act(zcopy(0, h, i)))

    zsends(lambda c: c.start())
    for copy in consts:
        copy.start()

    def zwait(side, h):
        plane = jnp.where(side == 0, r - 1 - h, depth + r + h)
        for i in range(2):
            pltpu.make_async_remote_copy(
                src_ref=img.at[i, plane], dst_ref=img.at[i, plane],
                send_sem=zs_sem.at[side, h, i], recv_sem=zr_sem.at[side, h, i],
                device_id=(slab, strip), device_id_type=MESH,
            ).wait_recv()

    def pack(plane):
        first = lax.broadcasted_iota(jnp.int32, (8, width), 0) < 4
        f0, m0 = img[0, plane, 0:8, :], img[1, plane, 0:8, :]
        f1, m1 = img[0, plane, rows - 8 : rows, :], img[1, plane, rows - 8 : rows, :]
        packout[0, plane] = jnp.where(first, m0, pltpu.roll(f0, 4, 0))
        packout[1, plane] = jnp.where(first, pltpu.roll(f1, 4, 0), m1)

    def ycopy(side):
        return pltpu.make_async_remote_copy(
            src_ref=packout.at[side, pl.ds(r, depth)], dst_ref=packin.at[1 - side, pl.ds(r, depth)],
            send_sem=ys_sem.at[side], recv_sem=yr_sem.at[1 - side],
            device_id=(slab, strip - 1 if side == 0 else strip + 1), device_id_type=MESH,
        )

    def fcopy(side, zside, h):
        plane = jnp.where(zside == 0, r - 1 - h, depth + r + h)
        return pltpu.make_async_remote_copy(
            src_ref=packout.at[side, plane], dst_ref=packin.at[1 - side, plane],
            send_sem=fs_sem.at[side, zside, h], recv_sem=fr_sem.at[1 - side, zside, h],
            device_id=(slab, strip - 1 if side == 0 else strip + 1), device_id_type=MESH,
        )

    def to_sides(act, make):
        pl.when(left)(lambda: act(make(0)))
        pl.when(right)(lambda: act(make(1)))

    def from_sides(make):
        pl.when(left)(lambda: make(1).wait_recv())
        pl.when(right)(lambda: make(0).wait_recv())

    for copy in own:
        copy.wait()

    def pack_own(p, carry):
        pack(p + r)
        return carry

    lax.fori_loop(0, depth, pack_own, 0)
    to_sides(lambda c: c.start(), ycopy)

    @pl.when(jnp.logical_not(left))
    def _():
        packin[0] = jnp.zeros_like(packin[0])

    @pl.when(jnp.logical_not(right))
    def _():
        packin[1] = jnp.zeros_like(packin[1])

    @pl.when(jnp.logical_not(down))
    def _():
        img[:, 0:r] = jnp.zeros((2, r, rows, width), jnp.float32)
        ysum[:, 0:r] = jnp.zeros((5, r, rows, width), jnp.float32)

    @pl.when(jnp.logical_not(up))
    def _():
        img[:, depth + r :] = jnp.zeros((2, r, rows, width), jnp.float32)
        ysum[:, depth + r :] = jnp.zeros((5, r, rows, width), jnp.float32)

    acc[...] = jnp.zeros_like(acc)

    chunk = 2 * LANE

    def rows_of(plane):
        first = lax.broadcasted_iota(jnp.int32, (8, chunk), 0) < 4
        filler = jnp.zeros((8, chunk), jnp.float32)
        for x in range(0, width, chunk):
            cols = slice(x, x + chunk)
            lo, hi = packin[0, plane, :, cols], packin[1, plane, :, cols]

            def around(i, low, high):
                t = pltpu.roll(jnp.concatenate([img[i, plane, :, cols], filler], axis=0), 4, 0)
                return jnp.concatenate(
                    [jnp.where(first, low, t[0:8]), t[8 : after - 8],
                     jnp.where(first, t[after - 8 :], high)], axis=0)

            f = around(0, lo, hi)
            m = around(1, pltpu.roll(lo, 4, 0), pltpu.roll(hi, 4, 0))
            for q, v in enumerate((f, m, f * f, m * m, f * m)):
                s = v + pltpu.roll(v, after - 1, 0)
                s = s + pltpu.roll(s, after - 2, 0)
                s = s + pltpu.roll(s, after - 4, 0)
                ysum[q, plane, :, cols] = s[0:rows] + v[8:after]
            diff = pltpu.roll(m, after - 5, 0) - pltpu.roll(m, after - 3, 0)
            grady[plane, :, cols] = diff[0:rows] * 0.5

    inv = 1.0 / float((2 * r + 1) ** 3)
    wide = width + LANE
    tail = jnp.zeros((8, LANE), jnp.float32)

    def force_of(z):
        for t in range(0, rows, 8):
            tile = slice(t, t + 8)
            sums = []
            for q in range(5):
                total = ysum[q, z, tile, :]
                for k in range(1, 2 * r + 1):
                    total = total + ysum[q, z + k, tile, :]
                total = jnp.concatenate([total, tail], axis=1)
                total = total + pltpu.roll(total, 1, 1) + pltpu.roll(total, wide - 1, 1)
                total = total + pltpu.roll(total, 3, 1) + pltpu.roll(total, wide - 3, 1)
                sums.append(total[:, 0:width] * inv)
            mean_f, mean_m, ff, mm, fm = sums
            cov = fm - mean_f * mean_m
            var_f = ff - mean_f * mean_f
            var_m = mm - mean_m * mean_m
            f, m = img[0, z + r, tile, :], img[1, z + r, tile, :]
            factor = 2.0 * cov / (var_f * var_m + EPS)
            resid = f - mean_f - cov / (var_m + EPS) * (m - mean_m)
            common = factor * resid
            mw = jnp.concatenate([m, tail], axis=1)
            gx = (pltpu.roll(mw, wide - 1, 1) - pltpu.roll(mw, 1, 1))[:, 0:width] * 0.5
            gz = (img[1, z + r + 1, tile, :] - img[1, z + r - 1, tile, :]) * 0.5
            gy = grady[z + r, tile, :]
            for k, g in enumerate((gz, gy, gx)):
                v = common * g
                for a in range(knots_z):
                    acc[a * 3 + k, tile, :] += v * fitz_ref[a, z]

    from_sides(ycopy)

    def own_rows(p, carry):
        rows_of(p + r)
        return carry

    lax.fori_loop(0, depth, own_rows, 0)

    @pl.when(jnp.logical_and(up, down))
    def _():
        def step(h, carry):
            zwait(0, h)
            pack(r - 1 - h)
            to_sides(lambda c: c.start(), lambda side: fcopy(side, 0, h))
            from_sides(lambda side: fcopy(side, 0, h))
            rows_of(r - 1 - h)
            return carry

        lax.fori_loop(0, r, step, 0)

    main = jnp.where(up, 1, 0)

    def place(s):
        return jnp.where(up, s, depth - 1 - s)

    def early(s, carry):
        force_of(place(s))
        return carry

    lax.fori_loop(0, depth - 2 * r, early, 0)

    def late(h, carry):
        plane = jnp.where(up, depth + r + h, r - 1 - h)
        zwait(main, h)
        pack(plane)
        to_sides(lambda c: c.start(), lambda side: fcopy(side, main, h))
        force_of(place(depth - 2 * r + h))
        from_sides(lambda side: fcopy(side, main, h))
        rows_of(plane)
        force_of(place(depth - r + h))
        return carry

    lax.fori_loop(0, r, late, 0)

    for copy in consts:
        copy.wait()
    reduced = dot(fity_ref[...], acc[...].reshape(knots_z * 3 * rows, width))
    block = dot(reduced, fitx[...])
    part[...] = block.reshape(part.shape)

    def pzcopy(side, dist):
        return pltpu.make_async_remote_copy(
            src_ref=part, dst_ref=part_z.at[1 - side, dist - 1],
            send_sem=pzs_sem.at[side, dist - 1], recv_sem=pzr_sem.at[1 - side, dist - 1],
            device_id=(slab - dist if side == 0 else slab + dist, strip), device_id_type=MESH,
        )

    def zfold(act_up, act_down):
        for dist in range(1, reach_z + 1):
            pl.when(slab < n_z - dist)(lambda: act_up(dist))
            pl.when(slab >= dist)(lambda: act_down(dist))

    zfold(lambda d: pzcopy(1, d).start(), lambda d: pzcopy(0, d).start())

    flat = (knots_y * pad_rows, ctl_pad)
    row_id = lax.broadcasted_iota(jnp.int32, flat, 0)
    inner_row = row_id % pad_rows
    knot_x = lax.broadcasted_iota(jnp.int32, flat, 1)
    used = (inner_row < knots_z * 3) & (knot_x < width // SPACING + 3)
    mass = (
        mass_of(slab * span_z + inner_row // 3, depth * n_z)
        * mass_of(strip * span_y + row_id // pad_rows, rows * n_y)
        * mass_of(knot_x, width)
    )
    weight = jnp.where(used, 1.0 / jnp.where(used, mass, 1.0), 0.0)

    zfold(lambda d: pzcopy(0, d).wait_recv(), lambda d: pzcopy(1, d).wait_recv())
    zfold(lambda d: pzcopy(1, d).wait_send(), lambda d: pzcopy(0, d).wait_send())
    for dist in range(1, reach_z + 1):
        offset = 3 * dist * span_z

        @pl.when(slab >= dist)
        def _():
            other = part_z[0, dist - 1].reshape(flat)
            moved = pltpu.roll(other, flat[0] - offset, 0)
            part[...] += jnp.where(inner_row < knots_z * 3 - offset, moved, 0.0).reshape(part.shape)

        @pl.when(slab < n_z - dist)
        def _():
            other = part_z[1, dist - 1].reshape(flat)
            moved = pltpu.roll(other, offset, 0)
            keep = (inner_row >= offset) & (inner_row < knots_z * 3)
            part[...] += jnp.where(keep, moved, 0.0).reshape(part.shape)

    def pycopy(side, dist):
        count = knots_y - dist * span_y
        start = 0 if side == 0 else dist * span_y
        return pltpu.make_async_remote_copy(
            src_ref=part.at[pl.ds(start, count)],
            dst_ref=part_y.at[1 - side, dist - 1, pl.ds(0, count)],
            send_sem=pys_sem.at[side, dist - 1], recv_sem=pyr_sem.at[1 - side, dist - 1],
            device_id=(slab, strip - dist if side == 0 else strip + dist), device_id_type=MESH,
        )

    def yfold(act_up, act_down):
        for dist in range(1, reach_y + 1):
            pl.when(strip < n_y - dist)(lambda: act_up(dist))
            pl.when(strip >= dist)(lambda: act_down(dist))

    yfold(lambda d: pycopy(1, d).start(), lambda d: pycopy(0, d).start())
    yfold(lambda d: pycopy(0, d).wait_recv(), lambda d: pycopy(1, d).wait_recv())
    yfold(lambda d: pycopy(1, d).wait_send(), lambda d: pycopy(0, d).wait_send())
    for dist in range(1, reach_y + 1):
        count = knots_y - dist * span_y

        @pl.when(strip >= dist)
        def _():
            part[0:count] += part_y[0, dist - 1, 0:count]

        @pl.when(strip < n_y - dist)
        def _():
            part[knots_y - count :] += part_y[1, dist - 1, 0:count]

    coef = part[...].reshape(flat) * weight
    lines = dot(evalzy_ref[...], coef)
    power = jnp.sum(lines * dot(lines, gram[...]))
    power_out[0] = jnp.full((8, LANE), power, jnp.float32)

    size = n_z * group

    def wcopy(step, stage):
        slot = step - 1 if stage == 0 else size - 1 + step - 1
        return pltpu.make_async_remote_copy(
            src_ref=power_out.at[stage], dst_ref=power_in.at[slot],
            send_sem=ws_sem.at[slot], recv_sem=wr_sem.at[slot],
            device_id=inner(step) if stage == 0 else outer(step), device_id_type=MESH,
        )

    for step in range(1, size):
        wcopy(step, 0).start()
    lines_per = lines.shape[0] // 3
    for k in range(3):
        field_ref[k] = dot(lines[k * lines_per : (k + 1) * lines_per], evalx[...]).reshape(
            depth, rows, width)
    total = power_out[0]
    for step in range(1, size):
        wcopy(step, 0).wait_recv()
    for step in range(1, size):
        total = total + power_in[step - 1]
    power_out[1] = total
    for step in range(1, groups):
        wcopy(step, 1).start()
    for step in range(1, size):
        wcopy(step, 0).wait_send()
    zsends(lambda c: c.wait_send())
    to_sides(lambda c: c.wait_send(), ycopy)

    def sent(zside):
        def step(h, carry):
            to_sides(lambda c: c.wait_send(), lambda side: fcopy(side, zside, h))
            return carry

        lax.fori_loop(0, r, step, 0)

    pl.when(up)(lambda: sent(1))
    pl.when(down)(lambda: sent(0))

    for step in range(1, groups):
        wcopy(step, 1).wait_recv()
    for step in range(1, groups):
        total = total + power_in[size - 1 + step - 1]
    for step in range(1, groups):
        wcopy(step, 1).wait_send()
    entries = float(3 * depth * rows * width) * n_z * n_y
    scale_ref[...] = 1.0 / (jnp.sqrt(total / entries) + 1e-06)


def shards(n_z, n_y, fixed, moving):
    depth, rows, width = fixed.shape
    r = RADIUS
    eval_z, fit_z = np_tables(depth)
    eval_y, fit_y = np_tables(rows)
    eval_x, fit_x = np_tables(width)
    knots_z, knots_y, knots_x = eval_z.shape[1], eval_y.shape[1], eval_x.shape[1]
    lines = knots_z * 3
    pad_rows = -(-lines // 8) * 8
    ctl_pad = -(-knots_x // LANE) * LANE
    f32 = np.float32
    fitx = np.zeros((width, ctl_pad))
    fitx[:, :knots_x] = fit_x
    evalx = np.zeros((ctl_pad, width))
    evalx[:knots_x] = eval_x.T
    gram = evalx @ evalx.T
    fity = np.zeros((knots_y, pad_rows, lines, rows))
    for line in range(lines):
        fity[:, line, line, :] = fit_y.T
    fity = fity.reshape(knots_y * pad_rows, lines * rows)
    evalzy = np.zeros((3, depth, rows, knots_y, pad_rows))
    for k in range(3):
        for a in range(knots_z):
            evalzy[k, :, :, :, a * 3 + k] = eval_z[:, a][:, None, None] * eval_y[None]
    evalzy = evalzy.reshape(3 * depth * rows, knots_y * pad_rows)
    group = group_size(n_y)
    slots = n_z * group - 1 + n_y // group - 1
    reach_z = min((depth // SPACING + 2) // (depth // SPACING), n_z - 1)
    reach_y = min((rows // SPACING + 2) // (rows // SPACING), n_y - 1)
    dma = pltpu.SemaphoreType.DMA
    vmem = functools.partial(pltpu.VMEM, dtype=jnp.float32)
    block = (knots_y, pad_rows, ctl_pad)
    anywhere = pl.BlockSpec(memory_space=pl.ANY)
    inside = pl.BlockSpec(memory_space=pltpu.VMEM)
    field, scale = pl.pallas_call(
        functools.partial(kernel, n_z, n_y, depth, rows, width, group, ctl_pad),
        out_shape=(
            jax.ShapeDtypeStruct((3, depth, rows, width), jnp.float32),
            jax.ShapeDtypeStruct((8, LANE), jnp.float32),
        ),
        in_specs=[pl.BlockSpec(memory_space=pltpu.SMEM)] + [anywhere] * 5 + [inside] * 2,
        out_specs=(inside, inside),
        scratch_shapes=[
            vmem((2, depth + 2 * r, rows, width)),
            vmem((2, depth + 2 * r, 8, width)),
            vmem((2, depth + 2 * r, 8, width)),
            vmem((5, depth + 2 * r, rows, width)),
            vmem((depth + 2 * r, rows, width)),
            vmem((lines, rows, width)),
            vmem((width, ctl_pad)),
            vmem((ctl_pad, width)),
            vmem((ctl_pad, ctl_pad)),
            vmem(block),
            vmem((2, reach_z) + block),
            vmem((2, reach_y) + block),
            vmem((2, 8, LANE)),
            vmem((slots, 8, LANE)),
            dma((2,)), dma((3,)),
            dma((2, r, 2)), dma((2, r, 2)),
            dma((2,)), dma((2,)),
            dma((2, 2, r)), dma((2, 2, r)),
            dma((2, reach_z)), dma((2, reach_z)),
            dma((2, reach_y)), dma((2, reach_y)),
            dma((slots,)), dma((slots,)),
        ],
        compiler_params=pltpu.CompilerParams(
            collective_id=0, has_side_effects=True, vmem_limit_bytes=48 * 1024 * 1024
        ),
        cost_estimate=pl.CostEstimate(flops=10**9, bytes_accessed=10**7, transcendentals=0),
    )(
        jnp.asarray(fit_z.T.astype(f32)), fixed, moving, jnp.asarray(fitx.astype(f32)),
        jnp.asarray(evalx.astype(f32)), jnp.asarray(gram.astype(f32)),
        jnp.asarray(fity.astype(f32)), jnp.asarray(evalzy.astype(f32)),
    )
    return field * scale[0, 0]


def solution(mesh):
    placed = (P("gz", "xy", None), P("gz", "xy", None))
    return jax.shard_map(
        functools.partial(shards, mesh.shape["gz"], mesh.shape["xy"]), mesh=mesh, in_specs=placed,
        out_specs=P(None, "gz", "xy", None), check_vma=False
    )
```

```python
import functools

import jax
import jax.numpy as jnp
import numpy as np
from jax import lax
from jax.experimental import pallas as pl
from jax.experimental.pallas import tpu as pltpu
from jax.sharding import PartitionSpec as P

RADIUS = 4
SPACING = 8
EPS = 1e-05
MESH = pl.DeviceIdType.MESH
LANE = 128


def np_basis(index, knot):
    span = index // SPACING
    t = (index - span * SPACING) / SPACING
    j = knot - span
    values = (
        (1 - t) ** 3 / 6,
        (3 * t**3 - 6 * t**2 + 4) / 6,
        (-3 * t**3 + 3 * t**2 + 3 * t + 1) / 6,
        t**3 / 6,
    )
    out = np.zeros(np.broadcast(index, knot).shape)
    for step in range(4):
        out = np.where(j == step, values[step], out)
    return out


def np_tables(extent):
    index = np.arange(extent)[:, None]
    value = np_basis(index, np.arange(extent // SPACING + 3)[None, :])
    return value, value**3 / (value**2).sum(axis=1, keepdims=True)


def energies():
    index = np.arange(SPACING)
    return [float((np_basis(index, np.full(SPACING, j)) ** 2).sum()) for j in range(4)]


def mass_of(knot, extent):
    total = jnp.zeros(knot.shape, jnp.float32)
    for j, energy in enumerate(energies()):
        start = knot - j
        total = total + jnp.where((start >= 0) & (start <= extent // SPACING - 1), energy, 0.0)
    return total


def group_size(count):
    size = 1
    while size * size < count and count % (size * 2) == 0:
        size *= 2
    return size


def dot(a, b):
    return jnp.dot(a, b, preferred_element_type=jnp.float32)


def halves(x):
    high = x.astype(jnp.bfloat16)
    return high, (x - high.astype(jnp.float32)).astype(jnp.bfloat16)


def np_halves(x):
    x = x.astype(np.float32)
    high = x.astype(jnp.bfloat16)
    return high, (x - high.astype(np.float32)).astype(jnp.bfloat16)


def dot3(a, b):
    return dot(a[0], b[0]) + (dot(a[1], b[0]) + dot(a[0], b[1]))


def kernel(
    n_z, n_y, depth, rows, width, group, ctl_pad,
    f_hbm, m_hbm, fitx_hbm, evalx_hbm, fity_hbm, evalzy_hbm, gram_hbm,
    field_ref, scale_ref,
    img, packout, packin, ysum, grady, acc, fitx, evalx, fity, evalzy, gram, fitz, part, part_z, part_y,
    power_out, power_in,
    own_sem, const_sem, zs_sem, zr_sem, ys_sem, yr_sem, fs_sem, fr_sem,
    pzs_sem, pzr_sem, pys_sem, pyr_sem, ws_sem, wr_sem,
):
    r = RADIUS
    slab, strip = lax.axis_index("gz"), lax.axis_index("xy")
    span_z, span_y = depth // SPACING, rows // SPACING
    knots_z, knots_y = span_z + 3, span_y + 3
    reach_z = min((span_z + 2) // span_z, n_z - 1)
    reach_y = min((span_y + 2) // span_y, n_y - 1)
    pad_rows = fity.shape[1] // knots_y
    up, down = slab < n_z - 1, slab > 0
    right, left = strip < n_y - 1, strip > 0
    after = rows + 2 * r

    own = [
        pltpu.make_async_copy(ref, img.at[i, pl.ds(r, depth)], own_sem.at[i])
        for i, ref in enumerate((f_hbm, m_hbm))
    ]
    consts = [
        pltpu.make_async_copy(src, dst, const_sem.at[i])
        for i, (src, dst) in enumerate(
            ((fitx_hbm, fitx), (evalx_hbm, evalx), (fity_hbm, fity), (evalzy_hbm, evalzy),
             (gram_hbm, gram))
        )
    ]
    for copy in own:
        copy.start()
    for copy in consts:
        copy.start()
    fit_table = np_tables(depth)[1]
    for a in range(knots_z):
        for z in range(depth):
            fitz[a, z] = jnp.float32(fit_table[z, a])

    barrier = pltpu.get_barrier_semaphore()
    lo_block = (strip // group) * group
    here = strip % group
    groups = n_y // group

    def beside(dist):
        if dist % group == 0:
            return []
        below = (strip >= dist) & (here < dist % group)
        above = (strip < n_y - dist) & (here >= group - dist % group)
        if dist > group:
            below, above = strip >= dist, strip < n_y - dist
        return [(below, strip - dist), (above, strip + dist)]

    def inner(step):
        place = (slab * group + here + step) % (n_z * group)
        return (place // group, lo_block + place % group)

    def outer(step):
        return (slab, (strip + step * group) % n_y)

    def greet(device):
        pl.semaphore_signal(barrier, inc=1, device_id=device, device_id_type=MESH)

    heard = n_z * group - 1 + groups - 1
    for step in range(1, n_z * group):
        greet(inner(step))
    for step in range(1, groups):
        greet(outer(step))
    for dist in range(1, reach_y + 1):
        for there, other in beside(dist):
            pl.when(there)(functools.partial(greet, (slab, other)))
            heard = heard + jnp.where(there, 1, 0)
    pl.semaphore_wait(barrier, heard)

    def zcopy(side, h, i):
        ref = (f_hbm, m_hbm)[i]
        src = h if side == 0 else depth - 1 - h
        dst = depth + r + h if side == 0 else r - 1 - h
        target = slab - 1 if side == 0 else slab + 1
        return pltpu.make_async_remote_copy(
            src_ref=ref.at[src], dst_ref=img.at[i, dst],
            send_sem=zs_sem.at[side, h, i], recv_sem=zr_sem.at[1 - side, h, i],
            device_id=(target, strip), device_id_type=MESH,
        )

    def zsends(act):
        for h in range(r):
            for i in range(2):
                pl.when(up)(lambda: act(zcopy(1, h, i)))
                pl.when(down)(lambda: act(zcopy(0, h, i)))

    zsends(lambda c: c.start())

    def zwait(side, h):
        plane = jnp.where(side == 0, r - 1 - h, depth + r + h)
        for i in range(2):
            pltpu.make_async_remote_copy(
                src_ref=img.at[i, plane], dst_ref=img.at[i, plane],
                send_sem=zs_sem.at[side, h, i], recv_sem=zr_sem.at[side, h, i],
                device_id=(slab, strip), device_id_type=MESH,
            ).wait_recv()

    def pack(plane):
        first = lax.broadcasted_iota(jnp.int32, (8, width), 0) < 4
        f0, m0 = img[0, plane, 0:8, :], img[1, plane, 0:8, :]
        f1, m1 = img[0, plane, rows - 8 : rows, :], img[1, plane, rows - 8 : rows, :]
        packout[0, plane] = jnp.where(first, m0, pltpu.roll(f0, 4, 0))
        packout[1, plane] = jnp.where(first, pltpu.roll(f1, 4, 0), m1)

    def ycopy(side):
        return pltpu.make_async_remote_copy(
            src_ref=packout.at[side, pl.ds(r, depth)], dst_ref=packin.at[1 - side, pl.ds(r, depth)],
            send_sem=ys_sem.at[side], recv_sem=yr_sem.at[1 - side],
            device_id=(slab, strip - 1 if side == 0 else strip + 1), device_id_type=MESH,
        )

    def fcopy(side, zside, h):
        plane = jnp.where(zside == 0, r - 1 - h, depth + r + h)
        return pltpu.make_async_remote_copy(
            src_ref=packout.at[side, plane], dst_ref=packin.at[1 - side, plane],
            send_sem=fs_sem.at[side, zside, h], recv_sem=fr_sem.at[1 - side, zside, h],
            device_id=(slab, strip - 1 if side == 0 else strip + 1), device_id_type=MESH,
        )

    def to_sides(act, make):
        pl.when(left)(lambda: act(make(0)))
        pl.when(right)(lambda: act(make(1)))

    def from_sides(make):
        pl.when(left)(lambda: make(1).wait_recv())
        pl.when(right)(lambda: make(0).wait_recv())

    for copy in own:
        copy.wait()

    def pack_own(p, carry):
        pack(p + r)
        return carry

    lax.fori_loop(0, depth, pack_own, 0)
    to_sides(lambda c: c.start(), ycopy)

    @pl.when(jnp.logical_not(left))
    def _():
        packin[0] = jnp.zeros_like(packin[0])

    @pl.when(jnp.logical_not(right))
    def _():
        packin[1] = jnp.zeros_like(packin[1])

    @pl.when(jnp.logical_not(down))
    def _():
        img[:, 0:r] = jnp.zeros((2, r, rows, width), jnp.float32)
        ysum[:, 0:r] = jnp.zeros((5, r, rows, width), jnp.float32)

    @pl.when(jnp.logical_not(up))
    def _():
        img[:, depth + r :] = jnp.zeros((2, r, rows, width), jnp.float32)
        ysum[:, depth + r :] = jnp.zeros((5, r, rows, width), jnp.float32)

    acc[...] = jnp.zeros_like(acc)

    chunk = 2 * LANE

    def rows_of(plane):
        first = lax.broadcasted_iota(jnp.int32, (8, chunk), 0) < 4
        filler = jnp.zeros((8, chunk), jnp.float32)
        for x in range(0, width, chunk):
            cols = slice(x, x + chunk)
            lo, hi = packin[0, plane, :, cols], packin[1, plane, :, cols]

            def around(i, low, high):
                t = pltpu.roll(jnp.concatenate([img[i, plane, :, cols], filler], axis=0), 4, 0)
                return jnp.concatenate(
                    [jnp.where(first, low, t[0:8]), t[8 : after - 8],
                     jnp.where(first, t[after - 8 :], high)], axis=0)

            f = around(0, lo, hi)
            m = around(1, pltpu.roll(lo, 4, 0), pltpu.roll(hi, 4, 0))
            for q, v in enumerate((f, m, f * f, m * m, f * m)):
                s = v + pltpu.roll(v, after - 1, 0)
                s = s + pltpu.roll(s, after - 2, 0)
                s = s + pltpu.roll(s, after - 4, 0)
                ysum[q, plane, :, cols] = s[0:rows] + v[8:after]
            diff = pltpu.roll(m, after - 5, 0) - pltpu.roll(m, after - 3, 0)
            grady[plane, :, cols] = diff[0:rows] * 0.5

    inv = 1.0 / float((2 * r + 1) ** 3)
    wide = width + LANE
    tail = jnp.zeros((8, LANE), jnp.float32)

    def force_of(z):
        for t in range(0, rows, 8):
            tile = slice(t, t + 8)
            sums = []
            for q in range(5):
                total = ysum[q, z, tile, :]
                for k in range(1, 2 * r + 1):
                    total = total + ysum[q, z + k, tile, :]
                total = jnp.concatenate([total, tail], axis=1)
                total = total + pltpu.roll(total, 1, 1) + pltpu.roll(total, wide - 1, 1)
                total = total + pltpu.roll(total, 3, 1) + pltpu.roll(total, wide - 3, 1)
                sums.append(total[:, 0:width] * inv)
            mean_f, mean_m, ff, mm, fm = sums
            cov = fm - mean_f * mean_m
            var_f = ff - mean_f * mean_f
            var_m = mm - mean_m * mean_m
            f, m = img[0, z + r, tile, :], img[1, z + r, tile, :]
            factor = 2.0 * cov / (var_f * var_m + EPS)
            resid = f - mean_f - cov / (var_m + EPS) * (m - mean_m)
            common = factor * resid
            mw = jnp.concatenate([m, tail], axis=1)
            gx = (pltpu.roll(mw, wide - 1, 1) - pltpu.roll(mw, 1, 1))[:, 0:width] * 0.5
            gz = (img[1, z + r + 1, tile, :] - img[1, z + r - 1, tile, :]) * 0.5
            gy = grady[z + r, tile, :]
            for k, g in enumerate((gz, gy, gx)):
                v = common * g
                for a in range(knots_z):
                    acc[a * 3 + k, tile, :] += v * fitz[a, z]

    from_sides(ycopy)

    def own_rows(p, carry):
        rows_of(p + r)
        return carry

    lax.fori_loop(0, depth, own_rows, 0)

    @pl.when(jnp.logical_and(up, down))
    def _():
        def step(h, carry):
            zwait(0, h)
            pack(r - 1 - h)
            to_sides(lambda c: c.start(), lambda side: fcopy(side, 0, h))
            from_sides(lambda side: fcopy(side, 0, h))
            rows_of(r - 1 - h)
            return carry

        lax.fori_loop(0, r, step, 0)

    main = jnp.where(up, 1, 0)

    def place(s):
        return jnp.where(up, s, depth - 1 - s)

    def early(s, carry):
        force_of(place(s))
        return carry

    lax.fori_loop(0, depth - 2 * r, early, 0)

    def late(h, carry):
        plane = jnp.where(up, depth + r + h, r - 1 - h)
        zwait(main, h)
        pack(plane)
        to_sides(lambda c: c.start(), lambda side: fcopy(side, main, h))
        force_of(place(depth - 2 * r + h))
        from_sides(lambda side: fcopy(side, main, h))
        rows_of(plane)
        force_of(place(depth - r + h))
        return carry

    lax.fori_loop(0, r, late, 0)

    for copy in consts:
        copy.wait()
    forces = halves(acc[...].reshape(knots_z * 3 * rows, width))
    reduced = halves(dot3((fity[0], fity[1]), forces))
    block = dot3(reduced, (fitx[0], fitx[1]))
    part[...] = block.reshape(part.shape)

    def pzcopy(side, dist):
        return pltpu.make_async_remote_copy(
            src_ref=part, dst_ref=part_z.at[1 - side, dist - 1],
            send_sem=pzs_sem.at[side, dist - 1], recv_sem=pzr_sem.at[1 - side, dist - 1],
            device_id=(slab - dist if side == 0 else slab + dist, strip), device_id_type=MESH,
        )

    def zfold(act_up, act_down):
        for dist in range(1, reach_z + 1):
            pl.when(slab < n_z - dist)(lambda: act_up(dist))
            pl.when(slab >= dist)(lambda: act_down(dist))

    zfold(lambda d: pzcopy(1, d).start(), lambda d: pzcopy(0, d).start())

    flat = (knots_y * pad_rows, ctl_pad)
    row_id = lax.broadcasted_iota(jnp.int32, flat, 0)
    inner_row = row_id % pad_rows
    knot_x = lax.broadcasted_iota(jnp.int32, flat, 1)
    used = (inner_row < knots_z * 3) & (knot_x < width // SPACING + 3)
    mass = (
        mass_of(slab * span_z + inner_row // 3, depth * n_z)
        * mass_of(strip * span_y + row_id // pad_rows, rows * n_y)
        * mass_of(knot_x, width)
    )
    weight = jnp.where(used, 1.0 / jnp.where(used, mass, 1.0), 0.0)

    zfold(lambda d: pzcopy(0, d).wait_recv(), lambda d: pzcopy(1, d).wait_recv())
    zfold(lambda d: pzcopy(1, d).wait_send(), lambda d: pzcopy(0, d).wait_send())
    for dist in range(1, reach_z + 1):
        offset = 3 * dist * span_z

        @pl.when(slab >= dist)
        def _():
            other = part_z[0, dist - 1].reshape(flat)
            moved = pltpu.roll(other, flat[0] - offset, 0)
            part[...] += jnp.where(inner_row < knots_z * 3 - offset, moved, 0.0).reshape(part.shape)

        @pl.when(slab < n_z - dist)
        def _():
            other = part_z[1, dist - 1].reshape(flat)
            moved = pltpu.roll(other, offset, 0)
            keep = (inner_row >= offset) & (inner_row < knots_z * 3)
            part[...] += jnp.where(keep, moved, 0.0).reshape(part.shape)

    def pycopy(side, dist):
        count = knots_y - dist * span_y
        start = 0 if side == 0 else dist * span_y
        return pltpu.make_async_remote_copy(
            src_ref=part.at[pl.ds(start, count)],
            dst_ref=part_y.at[1 - side, dist - 1, pl.ds(0, count)],
            send_sem=pys_sem.at[side, dist - 1], recv_sem=pyr_sem.at[1 - side, dist - 1],
            device_id=(slab, strip - dist if side == 0 else strip + dist), device_id_type=MESH,
        )

    def yfold(act_up, act_down):
        for dist in range(1, reach_y + 1):
            pl.when(strip < n_y - dist)(lambda: act_up(dist))
            pl.when(strip >= dist)(lambda: act_down(dist))

    yfold(lambda d: pycopy(1, d).start(), lambda d: pycopy(0, d).start())
    yfold(lambda d: pycopy(0, d).wait_recv(), lambda d: pycopy(1, d).wait_recv())
    yfold(lambda d: pycopy(1, d).wait_send(), lambda d: pycopy(0, d).wait_send())
    for dist in range(1, reach_y + 1):
        count = knots_y - dist * span_y

        @pl.when(strip >= dist)
        def _():
            part[0:count] += part_y[0, dist - 1, 0:count]

        @pl.when(strip < n_y - dist)
        def _():
            part[knots_y - count :] += part_y[1, dist - 1, 0:count]

    coef = part[...].reshape(flat) * weight
    lines = dot3(halves(coef), (evalx[0], evalx[1]))
    high, low = halves(lines)
    spread = jnp.concatenate([high, low, high], axis=0)
    power = jnp.sum(lines * dot(gram[...], spread))
    power_out[0] = jnp.full((8, LANE), power, jnp.float32)

    size = n_z * group

    def wcopy(step, stage):
        slot = step - 1 if stage == 0 else size - 1 + step - 1
        return pltpu.make_async_remote_copy(
            src_ref=power_out.at[stage], dst_ref=power_in.at[slot],
            send_sem=ws_sem.at[slot], recv_sem=wr_sem.at[slot],
            device_id=inner(step) if stage == 0 else outer(step), device_id_type=MESH,
        )

    for step in range(1, size):
        wcopy(step, 0).start()
    voxels = depth * rows
    for k in range(3):
        field_ref[k] = dot(evalzy[k * voxels : (k + 1) * voxels, :], spread).reshape(
            depth, rows, width)
    total = power_out[0]
    for step in range(1, size):
        wcopy(step, 0).wait_recv()
    for step in range(1, size):
        total = total + power_in[step - 1]
    power_out[1] = total
    for step in range(1, groups):
        wcopy(step, 1).start()
    for step in range(1, size):
        wcopy(step, 0).wait_send()
    zsends(lambda c: c.wait_send())
    to_sides(lambda c: c.wait_send(), ycopy)

    def sent(zside):
        def step(h, carry):
            to_sides(lambda c: c.wait_send(), lambda side: fcopy(side, zside, h))
            return carry

        lax.fori_loop(0, r, step, 0)

    pl.when(up)(lambda: sent(1))
    pl.when(down)(lambda: sent(0))

    for step in range(1, groups):
        wcopy(step, 1).wait_recv()
    for step in range(1, groups):
        total = total + power_in[size - 1 + step - 1]
    for step in range(1, groups):
        wcopy(step, 1).wait_send()
    entries = float(3 * depth * rows * width) * n_z * n_y
    scale = 1.0 / (jnp.sqrt(total / entries) + 1e-06)
    scale_ref[...] = jnp.broadcast_to(scale[0:1, 0:1], (rows, width))


def shards(n_z, n_y, fixed, moving):
    depth, rows, width = fixed.shape
    r = RADIUS
    eval_z = np_tables(depth)[0]
    eval_y, fit_y = np_tables(rows)
    eval_x, fit_x = np_tables(width)
    knots_z, knots_y, knots_x = eval_z.shape[1], eval_y.shape[1], eval_x.shape[1]
    lines = knots_z * 3
    pad_rows = -(-lines // 8) * 8
    ctl_pad = -(-knots_x // LANE) * LANE
    fitx = np.zeros((width, ctl_pad))
    fitx[:, :knots_x] = fit_x
    evalx = np.zeros((ctl_pad, width))
    evalx[:knots_x] = eval_x.T
    fity = np.zeros((knots_y, pad_rows, lines, rows))
    for line in range(lines):
        fity[:, line, line, :] = fit_y.T
    fity = fity.reshape(knots_y * pad_rows, lines * rows)
    evalzy = np.zeros((3, depth, rows, knots_y, pad_rows))
    for k in range(3):
        for a in range(knots_z):
            evalzy[k, :, :, :, a * 3 + k] = eval_z[:, a][:, None, None] * eval_y[None]
    evalzy = evalzy.reshape(3 * depth * rows, knots_y * pad_rows)
    gram = evalzy.T @ evalzy

    def thrice(table):
        high, low = np_halves(table)
        return jnp.asarray(np.concatenate([high, high, low], axis=1))

    def both(table):
        return jnp.asarray(np.stack(np_halves(table)))

    group = group_size(n_y)
    slots = n_z * group - 1 + n_y // group - 1
    reach_z = min((depth // SPACING + 2) // (depth // SPACING), n_z - 1)
    reach_y = min((rows // SPACING + 2) // (rows // SPACING), n_y - 1)
    dma = pltpu.SemaphoreType.DMA
    vmem = functools.partial(pltpu.VMEM, dtype=jnp.float32)
    half = functools.partial(pltpu.VMEM, dtype=jnp.bfloat16)
    lined = knots_y * pad_rows
    block = (knots_y, pad_rows, ctl_pad)
    anywhere = pl.BlockSpec(memory_space=pltpu.HBM)
    inside = pl.BlockSpec(memory_space=pltpu.VMEM)
    field, scale = pl.pallas_call(
        functools.partial(kernel, n_z, n_y, depth, rows, width, group, ctl_pad),
        out_shape=(
            jax.ShapeDtypeStruct((3, depth, rows, width), jnp.float32),
            jax.ShapeDtypeStruct((rows, width), jnp.float32),
        ),
        in_specs=[anywhere] * 7,
        out_specs=(inside, inside),
        scratch_shapes=[
            vmem((2, depth + 2 * r, rows, width)),
            vmem((2, depth + 2 * r, 8, width)),
            vmem((2, depth + 2 * r, 8, width)),
            vmem((5, depth + 2 * r, rows, width)),
            vmem((depth + 2 * r, rows, width)),
            vmem((lines, rows, width)),
            half((2, width, ctl_pad)),
            half((2, ctl_pad, width)),
            half((2, lined, lines * rows)),
            half((3 * depth * rows, 3 * lined)),
            half((lined, 3 * lined)),
            pltpu.SMEM((knots_z, depth), jnp.float32),
            vmem(block),
            vmem((2, reach_z) + block),
            vmem((2, reach_y) + block),
            vmem((2, 8, LANE)),
            vmem((slots, 8, LANE)),
            dma((2,)), dma((5,)),
            dma((2, r, 2)), dma((2, r, 2)),
            dma((2,)), dma((2,)),
            dma((2, 2, r)), dma((2, 2, r)),
            dma((2, reach_z)), dma((2, reach_z)),
            dma((2, reach_y)), dma((2, reach_y)),
            dma((slots,)), dma((slots,)),
        ],
        compiler_params=pltpu.CompilerParams(
            collective_id=0, has_side_effects=True, vmem_limit_bytes=60 * 1024 * 1024
        ),
        cost_estimate=pl.CostEstimate(flops=10**9, bytes_accessed=10**7, transcendentals=0),
    )(
        fixed, moving, both(fitx), both(evalx), both(fity), thrice(evalzy), thrice(gram),
    )
    return field * scale[None, None]


def solution(mesh):
    placed = (P("gz", "xy", None), P("gz", "xy", None))
    return jax.shard_map(
        functools.partial(shards, mesh.shape["gz"], mesh.shape["xy"]), mesh=mesh, in_specs=placed,
        out_specs=P(None, "gz", "xy", None), check_vma=False
    )
```

```python
import functools

import jax
import jax.numpy as jnp
import numpy as np
from jax import lax
from jax.experimental import pallas as pl
from jax.experimental.pallas import tpu as pltpu
from jax.sharding import PartitionSpec as P

RADIUS = 4
SPACING = 8
EPS = 1e-05
MESH = pl.DeviceIdType.MESH
LANE = 128


def np_basis(index, knot):
    span = index // SPACING
    t = (index - span * SPACING) / SPACING
    j = knot - span
    values = (
        (1 - t) ** 3 / 6,
        (3 * t**3 - 6 * t**2 + 4) / 6,
        (-3 * t**3 + 3 * t**2 + 3 * t + 1) / 6,
        t**3 / 6,
    )
    out = np.zeros(np.broadcast(index, knot).shape)
    for step in range(4):
        out = np.where(j == step, values[step], out)
    return out


def np_tables(extent):
    index = np.arange(extent)[:, None]
    value = np_basis(index, np.arange(extent // SPACING + 3)[None, :])
    return value, value**3 / (value**2).sum(axis=1, keepdims=True)


def energies():
    index = np.arange(SPACING)
    return [float((np_basis(index, np.full(SPACING, j)) ** 2).sum()) for j in range(4)]


def mass_of(knot, extent):
    total = jnp.zeros(knot.shape, jnp.float32)
    for j, energy in enumerate(energies()):
        start = knot - j
        total = total + jnp.where((start >= 0) & (start <= extent // SPACING - 1), energy, 0.0)
    return total


def group_size(count):
    size = 1
    while size * size < count and count % (size * 2) == 0:
        size *= 2
    return size


def dot(a, b):
    return jnp.dot(a, b, preferred_element_type=jnp.float32)


def halves(x):
    high = x.astype(jnp.bfloat16)
    return high, (x - high.astype(jnp.float32)).astype(jnp.bfloat16)


def np_halves(x):
    x = x.astype(np.float32)
    high = x.astype(jnp.bfloat16)
    return high, (x - high.astype(np.float32)).astype(jnp.bfloat16)


def dot3(a, b):
    return dot(a[0], b[0]) + (dot(a[1], b[0]) + dot(a[0], b[1]))


def kernel(
    n_z, n_y, depth, rows, width, group, ctl_pad,
    f_hbm, m_hbm, fitx_hbm, evalx_hbm, fity_hbm, evalzy_hbm, gram_hbm,
    field_ref, scale_ref,
    img, packout, packin, ysum, grady, acc, fitx, evalx, fity, evalzy, gram, fitz, part, part_z, part_y,
    power_out, power_in,
    own_sem, const_sem, zs_sem, zr_sem, ys_sem, yr_sem, fs_sem, fr_sem,
    pzs_sem, pzr_sem, pys_sem, pyr_sem, ws_sem, wr_sem,
):
    r = RADIUS
    slab, strip = lax.axis_index("gz"), lax.axis_index("xy")
    span_z, span_y = depth // SPACING, rows // SPACING
    knots_z, knots_y = span_z + 3, span_y + 3
    reach_z = min((span_z + 2) // span_z, n_z - 1)
    reach_y = min((span_y + 2) // span_y, n_y - 1)
    pad_rows = fity.shape[1] // knots_y
    up, down = slab < n_z - 1, slab > 0
    right, left = strip < n_y - 1, strip > 0
    after = rows + 2 * r

    own = [
        pltpu.make_async_copy(ref, img.at[i, pl.ds(r, depth)], own_sem.at[i])
        for i, ref in enumerate((f_hbm, m_hbm))
    ]
    consts = [
        pltpu.make_async_copy(src, dst, const_sem.at[i])
        for i, (src, dst) in enumerate(
            ((fitx_hbm, fitx), (evalx_hbm, evalx), (fity_hbm, fity), (evalzy_hbm, evalzy),
             (gram_hbm, gram))
        )
    ]
    for copy in own:
        copy.start()
    for copy in consts:
        copy.start()
    fit_table = np_tables(depth)[1]
    for a in range(knots_z):
        for z in range(depth):
            fitz[a, z] = jnp.float32(fit_table[z, a])

    barrier = pltpu.get_barrier_semaphore()
    lo_block = (strip // group) * group
    here = strip % group
    groups = n_y // group

    def beside(dist):
        if dist % group == 0:
            return []
        below = (strip >= dist) & (here < dist % group)
        above = (strip < n_y - dist) & (here >= group - dist % group)
        if dist > group:
            below, above = strip >= dist, strip < n_y - dist
        return [(below, strip - dist), (above, strip + dist)]

    def inner(step):
        place = (slab * group + here + step) % (n_z * group)
        return (place // group, lo_block + place % group)

    def outer(step):
        return (slab, (strip + step * group) % n_y)

    def greet(device):
        pl.semaphore_signal(barrier, inc=1, device_id=device, device_id_type=MESH)

    heard = n_z * group - 1 + groups - 1
    for step in range(1, n_z * group):
        greet(inner(step))
    for step in range(1, groups):
        greet(outer(step))
    for dist in range(1, reach_y + 1):
        for there, other in beside(dist):
            pl.when(there)(functools.partial(greet, (slab, other)))
            heard = heard + jnp.where(there, 1, 0)
    pl.semaphore_wait(barrier, heard)

    def zcopy(side, h, i):
        ref = (f_hbm, m_hbm)[i]
        src = h if side == 0 else depth - 1 - h
        dst = depth + r + h if side == 0 else r - 1 - h
        target = slab - 1 if side == 0 else slab + 1
        return pltpu.make_async_remote_copy(
            src_ref=ref.at[src], dst_ref=img.at[i, dst],
            send_sem=zs_sem.at[side, h, i], recv_sem=zr_sem.at[1 - side, h, i],
            device_id=(target, strip), device_id_type=MESH,
        )

    def zsends(act):
        for h in range(r):
            for i in range(2):
                pl.when(up)(lambda: act(zcopy(1, h, i)))
                pl.when(down)(lambda: act(zcopy(0, h, i)))

    zsends(lambda c: c.start())

    def zwait(side, h):
        plane = jnp.where(side == 0, r - 1 - h, depth + r + h)
        for i in range(2):
            pltpu.make_async_remote_copy(
                src_ref=img.at[i, plane], dst_ref=img.at[i, plane],
                send_sem=zs_sem.at[side, h, i], recv_sem=zr_sem.at[side, h, i],
                device_id=(slab, strip), device_id_type=MESH,
            ).wait_recv()

    def pack(plane):
        first = lax.broadcasted_iota(jnp.int32, (8, width), 0) < 4
        f0, m0 = img[0, plane, 0:8, :], img[1, plane, 0:8, :]
        f1, m1 = img[0, plane, rows - 8 : rows, :], img[1, plane, rows - 8 : rows, :]
        packout[0, plane] = jnp.where(first, m0, pltpu.roll(f0, 4, 0))
        packout[1, plane] = jnp.where(first, pltpu.roll(f1, 4, 0), m1)

    def ycopy(side):
        return pltpu.make_async_remote_copy(
            src_ref=packout.at[side, pl.ds(r, depth)], dst_ref=packin.at[1 - side, pl.ds(r, depth)],
            send_sem=ys_sem.at[side], recv_sem=yr_sem.at[1 - side],
            device_id=(slab, strip - 1 if side == 0 else strip + 1), device_id_type=MESH,
        )

    def fcopy(side, zside, h):
        plane = jnp.where(zside == 0, r - 1 - h, depth + r + h)
        return pltpu.make_async_remote_copy(
            src_ref=packout.at[side, plane], dst_ref=packin.at[1 - side, plane],
            send_sem=fs_sem.at[side, zside, h], recv_sem=fr_sem.at[1 - side, zside, h],
            device_id=(slab, strip - 1 if side == 0 else strip + 1), device_id_type=MESH,
        )

    def to_sides(act, make):
        pl.when(left)(lambda: act(make(0)))
        pl.when(right)(lambda: act(make(1)))

    def from_sides(make):
        pl.when(left)(lambda: make(1).wait_recv())
        pl.when(right)(lambda: make(0).wait_recv())

    for copy in own:
        copy.wait()

    def pack_own(p, carry):
        pack(p + r)
        return carry

    lax.fori_loop(0, depth, pack_own, 0)
    to_sides(lambda c: c.start(), ycopy)

    @pl.when(jnp.logical_not(left))
    def _():
        packin[0] = jnp.zeros_like(packin[0])

    @pl.when(jnp.logical_not(right))
    def _():
        packin[1] = jnp.zeros_like(packin[1])

    @pl.when(jnp.logical_not(down))
    def _():
        img[:, 0:r] = jnp.zeros((2, r, rows, width), jnp.float32)
        ysum[:, 0:r] = jnp.zeros((5, r, rows, width), jnp.float32)

    @pl.when(jnp.logical_not(up))
    def _():
        img[:, depth + r :] = jnp.zeros((2, r, rows, width), jnp.float32)
        ysum[:, depth + r :] = jnp.zeros((5, r, rows, width), jnp.float32)

    acc[...] = jnp.zeros_like(acc)

    chunk = 2 * LANE

    def rows_of(plane):
        first = lax.broadcasted_iota(jnp.int32, (8, chunk), 0) < 4
        filler = jnp.zeros((8, chunk), jnp.float32)
        for x in range(0, width, chunk):
            cols = slice(x, x + chunk)
            lo, hi = packin[0, plane, :, cols], packin[1, plane, :, cols]

            def around(i, low, high):
                t = pltpu.roll(jnp.concatenate([img[i, plane, :, cols], filler], axis=0), 4, 0)
                return jnp.concatenate(
                    [jnp.where(first, low, t[0:8]), t[8 : after - 8],
                     jnp.where(first, t[after - 8 :], high)], axis=0)

            f = around(0, lo, hi)
            m = around(1, pltpu.roll(lo, 4, 0), pltpu.roll(hi, 4, 0))
            for q, v in enumerate((f, m, f * f, m * m, f * m)):
                s = v + pltpu.roll(v, after - 1, 0)
                s = s + pltpu.roll(s, after - 2, 0)
                s = s + pltpu.roll(s, after - 4, 0)
                ysum[q, plane, :, cols] = s[0:rows] + v[8:after]
            diff = pltpu.roll(m, after - 5, 0) - pltpu.roll(m, after - 3, 0)
            grady[plane, :, cols] = diff[0:rows] * 0.5

    inv = 1.0 / float((2 * r + 1) ** 3)
    wide = width + LANE
    tail = jnp.zeros((8, LANE), jnp.float32)

    def force_of(z):
        for t in range(0, rows, 8):
            tile = slice(t, t + 8)
            sums = []
            for q in range(5):
                total = ysum[q, z, tile, :]
                for k in range(1, 2 * r + 1):
                    total = total + ysum[q, z + k, tile, :]
                total = jnp.concatenate([total, tail], axis=1)
                total = total + pltpu.roll(total, 1, 1) + pltpu.roll(total, wide - 1, 1)
                total = total + pltpu.roll(total, 3, 1) + pltpu.roll(total, wide - 3, 1)
                sums.append(total[:, 0:width] * inv)
            mean_f, mean_m, ff, mm, fm = sums
            cov = fm - mean_f * mean_m
            var_f = ff - mean_f * mean_f
            var_m = mm - mean_m * mean_m
            f, m = img[0, z + r, tile, :], img[1, z + r, tile, :]
            factor = 2.0 * cov / (var_f * var_m + EPS)
            resid = f - mean_f - cov / (var_m + EPS) * (m - mean_m)
            common = factor * resid
            mw = jnp.concatenate([m, tail], axis=1)
            gx = (pltpu.roll(mw, wide - 1, 1) - pltpu.roll(mw, 1, 1))[:, 0:width] * 0.5
            gz = (img[1, z + r + 1, tile, :] - img[1, z + r - 1, tile, :]) * 0.5
            gy = grady[z + r, tile, :]
            for k, g in enumerate((gz, gy, gx)):
                v = common * g
                for a in range(knots_z):
                    acc[a * 3 + k, tile, :] += v * fitz[a, z]

    from_sides(ycopy)

    def own_rows(p, carry):
        rows_of(p + r)
        return carry

    lax.fori_loop(0, depth, own_rows, 0)

    @pl.when(jnp.logical_and(up, down))
    def _():
        def step(h, carry):
            zwait(0, h)
            pack(r - 1 - h)
            to_sides(lambda c: c.start(), lambda side: fcopy(side, 0, h))
            from_sides(lambda side: fcopy(side, 0, h))
            rows_of(r - 1 - h)
            return carry

        lax.fori_loop(0, r, step, 0)

    main = jnp.where(up, 1, 0)

    def place(s):
        return jnp.where(up, s, depth - 1 - s)

    def early(s, carry):
        force_of(place(s))
        return carry

    lax.fori_loop(0, depth - r, early, 0)

    def pass_on(h, carry):
        zwait(main, h)
        pack(jnp.where(up, depth + r + h, r - 1 - h))
        to_sides(lambda c: c.start(), lambda side: fcopy(side, main, h))
        return carry

    lax.fori_loop(0, r, pass_on, 0)

    def late(h, carry):
        from_sides(lambda side: fcopy(side, main, h))
        rows_of(jnp.where(up, depth + r + h, r - 1 - h))
        force_of(place(depth - r + h))
        return carry

    lax.fori_loop(0, r, late, 0)

    for copy in consts:
        copy.wait()
    forces = halves(acc[...].reshape(knots_z * 3 * rows, width))
    reduced = halves(dot3((fity[0], fity[1]), forces))
    block = dot3(reduced, (fitx[0], fitx[1]))
    part[...] = block.reshape(part.shape)

    def pzcopy(side, dist):
        return pltpu.make_async_remote_copy(
            src_ref=part, dst_ref=part_z.at[1 - side, dist - 1],
            send_sem=pzs_sem.at[side, dist - 1], recv_sem=pzr_sem.at[1 - side, dist - 1],
            device_id=(slab - dist if side == 0 else slab + dist, strip), device_id_type=MESH,
        )

    def zfold(act_up, act_down):
        for dist in range(1, reach_z + 1):
            pl.when(slab < n_z - dist)(lambda: act_up(dist))
            pl.when(slab >= dist)(lambda: act_down(dist))

    zfold(lambda d: pzcopy(1, d).start(), lambda d: pzcopy(0, d).start())

    flat = (knots_y * pad_rows, ctl_pad)
    row_id = lax.broadcasted_iota(jnp.int32, flat, 0)
    inner_row = row_id % pad_rows
    knot_x = lax.broadcasted_iota(jnp.int32, flat, 1)
    used = (inner_row < knots_z * 3) & (knot_x < width // SPACING + 3)
    mass = (
        mass_of(slab * span_z + inner_row // 3, depth * n_z)
        * mass_of(strip * span_y + row_id // pad_rows, rows * n_y)
        * mass_of(knot_x, width)
    )
    weight = jnp.where(used, 1.0 / jnp.where(used, mass, 1.0), 0.0)

    zfold(lambda d: pzcopy(0, d).wait_recv(), lambda d: pzcopy(1, d).wait_recv())
    zfold(lambda d: pzcopy(1, d).wait_send(), lambda d: pzcopy(0, d).wait_send())
    for dist in range(1, reach_z + 1):
        offset = 3 * dist * span_z

        @pl.when(slab >= dist)
        def _():
            other = part_z[0, dist - 1].reshape(flat)
            moved = pltpu.roll(other, flat[0] - offset, 0)
            part[...] += jnp.where(inner_row < knots_z * 3 - offset, moved, 0.0).reshape(part.shape)

        @pl.when(slab < n_z - dist)
        def _():
            other = part_z[1, dist - 1].reshape(flat)
            moved = pltpu.roll(other, offset, 0)
            keep = (inner_row >= offset) & (inner_row < knots_z * 3)
            part[...] += jnp.where(keep, moved, 0.0).reshape(part.shape)

    def pycopy(side, dist):
        count = knots_y - dist * span_y
        start = 0 if side == 0 else dist * span_y
        return pltpu.make_async_remote_copy(
            src_ref=part.at[pl.ds(start, count)],
            dst_ref=part_y.at[1 - side, dist - 1, pl.ds(0, count)],
            send_sem=pys_sem.at[side, dist - 1], recv_sem=pyr_sem.at[1 - side, dist - 1],
            device_id=(slab, strip - dist if side == 0 else strip + dist), device_id_type=MESH,
        )

    def yfold(act_up, act_down):
        for dist in range(1, reach_y + 1):
            pl.when(strip < n_y - dist)(lambda: act_up(dist))
            pl.when(strip >= dist)(lambda: act_down(dist))

    yfold(lambda d: pycopy(1, d).start(), lambda d: pycopy(0, d).start())
    yfold(lambda d: pycopy(0, d).wait_recv(), lambda d: pycopy(1, d).wait_recv())
    yfold(lambda d: pycopy(1, d).wait_send(), lambda d: pycopy(0, d).wait_send())
    for dist in range(1, reach_y + 1):
        count = knots_y - dist * span_y

        @pl.when(strip >= dist)
        def _():
            part[0:count] += part_y[0, dist - 1, 0:count]

        @pl.when(strip < n_y - dist)
        def _():
            part[knots_y - count :] += part_y[1, dist - 1, 0:count]

    coef = part[...].reshape(flat) * weight
    lines = dot3(halves(coef), (evalx[0], evalx[1]))
    high, low = halves(lines)
    spread = jnp.concatenate([high, low, high], axis=0)
    power = jnp.sum(lines * dot(gram[...], spread))
    power_out[0] = jnp.full((8, LANE), power, jnp.float32)

    size = n_z * group

    def wcopy(step, stage):
        slot = step - 1 if stage == 0 else size - 1 + step - 1
        return pltpu.make_async_remote_copy(
            src_ref=power_out.at[stage], dst_ref=power_in.at[slot],
            send_sem=ws_sem.at[slot], recv_sem=wr_sem.at[slot],
            device_id=inner(step) if stage == 0 else outer(step), device_id_type=MESH,
        )

    for step in range(1, size):
        wcopy(step, 0).start()
    voxels = depth * rows
    for k in range(3):
        field_ref[k] = dot(evalzy[k * voxels : (k + 1) * voxels, :], spread).reshape(
            depth, rows, width)
    total = power_out[0]
    for step in range(1, size):
        wcopy(step, 0).wait_recv()
    for step in range(1, size):
        total = total + power_in[step - 1]
    power_out[1] = total
    for step in range(1, groups):
        wcopy(step, 1).start()
    for step in range(1, size):
        wcopy(step, 0).wait_send()
    zsends(lambda c: c.wait_send())
    to_sides(lambda c: c.wait_send(), ycopy)

    def sent(zside):
        def step(h, carry):
            to_sides(lambda c: c.wait_send(), lambda side: fcopy(side, zside, h))
            return carry

        lax.fori_loop(0, r, step, 0)

    pl.when(up)(lambda: sent(1))
    pl.when(down)(lambda: sent(0))

    for step in range(1, groups):
        wcopy(step, 1).wait_recv()
    for step in range(1, groups):
        total = total + power_in[size - 1 + step - 1]
    for step in range(1, groups):
        wcopy(step, 1).wait_send()
    entries = float(3 * depth * rows * width) * n_z * n_y
    scale = 1.0 / (jnp.sqrt(total / entries) + 1e-06)
    scale_ref[...] = jnp.broadcast_to(scale[0:1, 0:1], (rows, width))


def shards(n_z, n_y, fixed, moving):
    depth, rows, width = fixed.shape
    r = RADIUS
    eval_z = np_tables(depth)[0]
    eval_y, fit_y = np_tables(rows)
    eval_x, fit_x = np_tables(width)
    knots_z, knots_y, knots_x = eval_z.shape[1], eval_y.shape[1], eval_x.shape[1]
    lines = knots_z * 3
    pad_rows = -(-lines // 8) * 8
    ctl_pad = -(-knots_x // LANE) * LANE
    fitx = np.zeros((width, ctl_pad))
    fitx[:, :knots_x] = fit_x
    evalx = np.zeros((ctl_pad, width))
    evalx[:knots_x] = eval_x.T
    fity = np.zeros((knots_y, pad_rows, lines, rows))
    for line in range(lines):
        fity[:, line, line, :] = fit_y.T
    fity = fity.reshape(knots_y * pad_rows, lines * rows)
    evalzy = np.zeros((3, depth, rows, knots_y, pad_rows))
    for k in range(3):
        for a in range(knots_z):
            evalzy[k, :, :, :, a * 3 + k] = eval_z[:, a][:, None, None] * eval_y[None]
    evalzy = evalzy.reshape(3 * depth * rows, knots_y * pad_rows)
    gram = evalzy.T @ evalzy

    def thrice(table):
        high, low = np_halves(table)
        return jnp.asarray(np.concatenate([high, high, low], axis=1))

    def both(table):
        return jnp.asarray(np.stack(np_halves(table)))

    group = group_size(n_y)
    slots = n_z * group - 1 + n_y // group - 1
    reach_z = min((depth // SPACING + 2) // (depth // SPACING), n_z - 1)
    reach_y = min((rows // SPACING + 2) // (rows // SPACING), n_y - 1)
    dma = pltpu.SemaphoreType.DMA
    vmem = functools.partial(pltpu.VMEM, dtype=jnp.float32)
    half = functools.partial(pltpu.VMEM, dtype=jnp.bfloat16)
    lined = knots_y * pad_rows
    block = (knots_y, pad_rows, ctl_pad)
    anywhere = pl.BlockSpec(memory_space=pltpu.HBM)
    inside = pl.BlockSpec(memory_space=pltpu.VMEM)
    field, scale = pl.pallas_call(
        functools.partial(kernel, n_z, n_y, depth, rows, width, group, ctl_pad),
        out_shape=(
            jax.ShapeDtypeStruct((3, depth, rows, width), jnp.float32),
            jax.ShapeDtypeStruct((rows, width), jnp.float32),
        ),
        in_specs=[anywhere] * 7,
        out_specs=(inside, inside),
        scratch_shapes=[
            vmem((2, depth + 2 * r, rows, width)),
            vmem((2, depth + 2 * r, 8, width)),
            vmem((2, depth + 2 * r, 8, width)),
            vmem((5, depth + 2 * r, rows, width)),
            vmem((depth + 2 * r, rows, width)),
            vmem((lines, rows, width)),
            half((2, width, ctl_pad)),
            half((2, ctl_pad, width)),
            half((2, lined, lines * rows)),
            half((3 * depth * rows, 3 * lined)),
            half((lined, 3 * lined)),
            pltpu.SMEM((knots_z, depth), jnp.float32),
            vmem(block),
            vmem((2, reach_z) + block),
            vmem((2, reach_y) + block),
            vmem((2, 8, LANE)),
            vmem((slots, 8, LANE)),
            dma((2,)), dma((5,)),
            dma((2, r, 2)), dma((2, r, 2)),
            dma((2,)), dma((2,)),
            dma((2, 2, r)), dma((2, 2, r)),
            dma((2, reach_z)), dma((2, reach_z)),
            dma((2, reach_y)), dma((2, reach_y)),
            dma((slots,)), dma((slots,)),
        ],
        compiler_params=pltpu.CompilerParams(
            collective_id=0, has_side_effects=True, vmem_limit_bytes=60 * 1024 * 1024
        ),
        cost_estimate=pl.CostEstimate(flops=10**9, bytes_accessed=10**7, transcendentals=0),
    )(
        fixed, moving, both(fitx), both(evalx), both(fity), thrice(evalzy), thrice(gram),
    )
    return field * scale[None, None]


def solution(mesh):
    placed = (P("gz", "xy", None), P("gz", "xy", None))
    return jax.shard_map(
        functools.partial(shards, mesh.shape["gz"], mesh.shape["xy"]), mesh=mesh, in_specs=placed,
        out_specs=P(None, "gz", "xy", None), check_vma=False
    )
```

```python
import functools

import jax
import jax.numpy as jnp
import numpy as np
from jax import lax
from jax.experimental import pallas as pl
from jax.experimental.pallas import tpu as pltpu
from jax.sharding import PartitionSpec as P

RADIUS = 4
SPACING = 8
EPS = 1e-05
MESH = pl.DeviceIdType.MESH
LANE = 128


def np_basis(index, knot):
    span = index // SPACING
    t = (index - span * SPACING) / SPACING
    j = knot - span
    values = (
        (1 - t) ** 3 / 6,
        (3 * t**3 - 6 * t**2 + 4) / 6,
        (-3 * t**3 + 3 * t**2 + 3 * t + 1) / 6,
        t**3 / 6,
    )
    out = np.zeros(np.broadcast(index, knot).shape)
    for step in range(4):
        out = np.where(j == step, values[step], out)
    return out


def np_tables(extent):
    index = np.arange(extent)[:, None]
    value = np_basis(index, np.arange(extent // SPACING + 3)[None, :])
    return value, value**3 / (value**2).sum(axis=1, keepdims=True)


def energies():
    index = np.arange(SPACING)
    return [float((np_basis(index, np.full(SPACING, j)) ** 2).sum()) for j in range(4)]


def mass_of(knot, extent):
    total = jnp.zeros(knot.shape, jnp.float32)
    for j, energy in enumerate(energies()):
        start = knot - j
        total = total + jnp.where((start >= 0) & (start <= extent // SPACING - 1), energy, 0.0)
    return total


def group_size(count):
    size = 1
    while size * size < count and count % (size * 2) == 0:
        size *= 2
    return size


def dot(a, b):
    return jnp.dot(a, b, preferred_element_type=jnp.float32)


def halves(x):
    high = x.astype(jnp.bfloat16)
    return high, (x - high.astype(jnp.float32)).astype(jnp.bfloat16)


def np_halves(x):
    x = x.astype(np.float32)
    high = x.astype(jnp.bfloat16)
    return high, (x - high.astype(np.float32)).astype(jnp.bfloat16)


def dot3(a, b):
    return dot(a[0], b[0]) + (dot(a[1], b[0]) + dot(a[0], b[1]))


def kernel(
    n_z, n_y, depth, rows, width, group, ctl_pad,
    f_hbm, m_hbm, fitx_hbm, evalx_hbm, fity_hbm, gram_hbm,
    spread_ref,
    img, packout, packin, ysum, grady, acc, fitx, evalx, fity, gram, fitz, part, part_z, part_y,
    power_out, power_in,
    own_sem, const_sem, zs_sem, zr_sem, ys_sem, yr_sem, fs_sem, fr_sem,
    pzs_sem, pzr_sem, pys_sem, pyr_sem, ws_sem, wr_sem,
):
    r = RADIUS
    slab, strip = lax.axis_index("gz"), lax.axis_index("xy")
    span_z, span_y = depth // SPACING, rows // SPACING
    knots_z, knots_y = span_z + 3, span_y + 3
    reach_z = min((span_z + 2) // span_z, n_z - 1)
    reach_y = min((span_y + 2) // span_y, n_y - 1)
    pad_rows = fity.shape[1] // knots_y
    up, down = slab < n_z - 1, slab > 0
    right, left = strip < n_y - 1, strip > 0
    after = rows + 2 * r

    own = [
        pltpu.make_async_copy(ref, img.at[i, pl.ds(r, depth)], own_sem.at[i])
        for i, ref in enumerate((f_hbm, m_hbm))
    ]
    consts = [
        pltpu.make_async_copy(src, dst, const_sem.at[i])
        for i, (src, dst) in enumerate(
            ((fitx_hbm, fitx), (evalx_hbm, evalx), (fity_hbm, fity), (gram_hbm, gram))
        )
    ]
    for copy in own:
        copy.start()
    for copy in consts:
        copy.start()
    fit_table = np_tables(depth)[1]
    for a in range(knots_z):
        for z in range(depth):
            fitz[a, z] = jnp.float32(fit_table[z, a])

    barrier = pltpu.get_barrier_semaphore()
    lo_block = (strip // group) * group
    here = strip % group
    groups = n_y // group

    def beside(dist):
        if dist % group == 0:
            return []
        below = (strip >= dist) & (here < dist % group)
        above = (strip < n_y - dist) & (here >= group - dist % group)
        if dist > group:
            below, above = strip >= dist, strip < n_y - dist
        return [(below, strip - dist), (above, strip + dist)]

    def inner(step):
        place = (slab * group + here + step) % (n_z * group)
        return (place // group, lo_block + place % group)

    def outer(step):
        return (slab, (strip + step * group) % n_y)

    def greet(device):
        pl.semaphore_signal(barrier, inc=1, device_id=device, device_id_type=MESH)

    heard = n_z * group - 1 + groups - 1
    for step in range(1, n_z * group):
        greet(inner(step))
    for step in range(1, groups):
        greet(outer(step))
    for dist in range(1, reach_y + 1):
        for there, other in beside(dist):
            pl.when(there)(functools.partial(greet, (slab, other)))
            heard = heard + jnp.where(there, 1, 0)
    pl.semaphore_wait(barrier, heard)

    def zcopy(side, h, i):
        ref = (f_hbm, m_hbm)[i]
        src = h if side == 0 else depth - 1 - h
        dst = depth + r + h if side == 0 else r - 1 - h
        target = slab - 1 if side == 0 else slab + 1
        return pltpu.make_async_remote_copy(
            src_ref=ref.at[src], dst_ref=img.at[i, dst],
            send_sem=zs_sem.at[side, h, i], recv_sem=zr_sem.at[1 - side, h, i],
            device_id=(target, strip), device_id_type=MESH,
        )

    def zsends(act):
        for h in range(r):
            for i in range(2):
                pl.when(up)(lambda: act(zcopy(1, h, i)))
                pl.when(down)(lambda: act(zcopy(0, h, i)))

    zsends(lambda c: c.start())

    def zwait(side, h):
        plane = jnp.where(side == 0, r - 1 - h, depth + r + h)
        for i in range(2):
            pltpu.make_async_remote_copy(
                src_ref=img.at[i, plane], dst_ref=img.at[i, plane],
                send_sem=zs_sem.at[side, h, i], recv_sem=zr_sem.at[side, h, i],
                device_id=(slab, strip), device_id_type=MESH,
            ).wait_recv()

    def pack(plane):
        first = lax.broadcasted_iota(jnp.int32, (8, width), 0) < 4
        f0, m0 = img[0, plane, 0:8, :], img[1, plane, 0:8, :]
        f1, m1 = img[0, plane, rows - 8 : rows, :], img[1, plane, rows - 8 : rows, :]
        packout[0, plane] = jnp.where(first, m0, pltpu.roll(f0, 4, 0))
        packout[1, plane] = jnp.where(first, pltpu.roll(f1, 4, 0), m1)

    def ycopy(side):
        return pltpu.make_async_remote_copy(
            src_ref=packout.at[side, pl.ds(r, depth)], dst_ref=packin.at[1 - side, pl.ds(r, depth)],
            send_sem=ys_sem.at[side], recv_sem=yr_sem.at[1 - side],
            device_id=(slab, strip - 1 if side == 0 else strip + 1), device_id_type=MESH,
        )

    def fcopy(side, zside, h):
        plane = jnp.where(zside == 0, r - 1 - h, depth + r + h)
        return pltpu.make_async_remote_copy(
            src_ref=packout.at[side, plane], dst_ref=packin.at[1 - side, plane],
            send_sem=fs_sem.at[side, zside, h], recv_sem=fr_sem.at[1 - side, zside, h],
            device_id=(slab, strip - 1 if side == 0 else strip + 1), device_id_type=MESH,
        )

    def to_sides(act, make):
        pl.when(left)(lambda: act(make(0)))
        pl.when(right)(lambda: act(make(1)))

    def from_sides(make):
        pl.when(left)(lambda: make(1).wait_recv())
        pl.when(right)(lambda: make(0).wait_recv())

    for copy in own:
        copy.wait()

    def pack_own(p, carry):
        pack(p + r)
        return carry

    lax.fori_loop(0, depth, pack_own, 0)
    to_sides(lambda c: c.start(), ycopy)

    @pl.when(jnp.logical_not(left))
    def _():
        packin[0] = jnp.zeros_like(packin[0])

    @pl.when(jnp.logical_not(right))
    def _():
        packin[1] = jnp.zeros_like(packin[1])

    @pl.when(jnp.logical_not(down))
    def _():
        img[:, 0:r] = jnp.zeros((2, r, rows, width), jnp.float32)
        ysum[:, 0:r] = jnp.zeros((5, r, rows, width), jnp.float32)

    @pl.when(jnp.logical_not(up))
    def _():
        img[:, depth + r :] = jnp.zeros((2, r, rows, width), jnp.float32)
        ysum[:, depth + r :] = jnp.zeros((5, r, rows, width), jnp.float32)

    acc[...] = jnp.zeros_like(acc)

    chunk = 2 * LANE

    def rows_of(plane):
        first = lax.broadcasted_iota(jnp.int32, (8, chunk), 0) < 4
        filler = jnp.zeros((8, chunk), jnp.float32)
        for x in range(0, width, chunk):
            cols = slice(x, x + chunk)
            lo, hi = packin[0, plane, :, cols], packin[1, plane, :, cols]

            def around(i, low, high):
                t = pltpu.roll(jnp.concatenate([img[i, plane, :, cols], filler], axis=0), 4, 0)
                return jnp.concatenate(
                    [jnp.where(first, low, t[0:8]), t[8 : after - 8],
                     jnp.where(first, t[after - 8 :], high)], axis=0)

            f = around(0, lo, hi)
            m = around(1, pltpu.roll(lo, 4, 0), pltpu.roll(hi, 4, 0))
            for q, v in enumerate((f, m, f * f, m * m, f * m)):
                s = v + pltpu.roll(v, after - 1, 0)
                s = s + pltpu.roll(s, after - 2, 0)
                s = s + pltpu.roll(s, after - 4, 0)
                ysum[q, plane, :, cols] = s[0:rows] + v[8:after]
            diff = pltpu.roll(m, after - 5, 0) - pltpu.roll(m, after - 3, 0)
            grady[plane, :, cols] = diff[0:rows] * 0.5

    inv = 1.0 / float((2 * r + 1) ** 3)
    wide = width + LANE
    tail = jnp.zeros((8, LANE), jnp.float32)

    def force_of(z):
        for t in range(0, rows, 8):
            tile = slice(t, t + 8)
            sums = []
            for q in range(5):
                total = ysum[q, z, tile, :]
                for k in range(1, 2 * r + 1):
                    total = total + ysum[q, z + k, tile, :]
                total = jnp.concatenate([total, tail], axis=1)
                total = total + pltpu.roll(total, 1, 1) + pltpu.roll(total, wide - 1, 1)
                total = total + pltpu.roll(total, 3, 1) + pltpu.roll(total, wide - 3, 1)
                sums.append(total[:, 0:width] * inv)
            mean_f, mean_m, ff, mm, fm = sums
            cov = fm - mean_f * mean_m
            var_f = ff - mean_f * mean_f
            var_m = mm - mean_m * mean_m
            f, m = img[0, z + r, tile, :], img[1, z + r, tile, :]
            factor = 2.0 * cov / (var_f * var_m + EPS)
            resid = f - mean_f - cov / (var_m + EPS) * (m - mean_m)
            common = factor * resid
            mw = jnp.concatenate([m, tail], axis=1)
            gx = (pltpu.roll(mw, wide - 1, 1) - pltpu.roll(mw, 1, 1))[:, 0:width] * 0.5
            gz = (img[1, z + r + 1, tile, :] - img[1, z + r - 1, tile, :]) * 0.5
            gy = grady[z + r, tile, :]
            for k, g in enumerate((gz, gy, gx)):
                v = common * g
                for a in range(knots_z):
                    acc[a * 3 + k, tile, :] += v * fitz[a, z]

    from_sides(ycopy)

    def own_rows(p, carry):
        rows_of(p + r)
        return carry

    lax.fori_loop(0, depth, own_rows, 0)

    @pl.when(jnp.logical_and(up, down))
    def _():
        def step(h, carry):
            zwait(0, h)
            pack(r - 1 - h)
            to_sides(lambda c: c.start(), lambda side: fcopy(side, 0, h))
            from_sides(lambda side: fcopy(side, 0, h))
            rows_of(r - 1 - h)
            return carry

        lax.fori_loop(0, r, step, 0)

    main = jnp.where(up, 1, 0)

    def place(s):
        return jnp.where(up, s, depth - 1 - s)

    def early(s, carry):
        force_of(place(s))
        return carry

    lax.fori_loop(0, depth - r, early, 0)

    def pass_on(h, carry):
        zwait(main, h)
        pack(jnp.where(up, depth + r + h, r - 1 - h))
        to_sides(lambda c: c.start(), lambda side: fcopy(side, main, h))
        return carry

    pass_on(0, 0)

    def late(h, carry):
        @pl.when(h + 1 < r)
        def _():
            pass_on(h + 1, 0)

        from_sides(lambda side: fcopy(side, main, h))
        rows_of(jnp.where(up, depth + r + h, r - 1 - h))
        force_of(place(depth - r + h))
        return carry

    lax.fori_loop(0, r, late, 0)

    for copy in consts:
        copy.wait()
    forces = halves(acc[...].reshape(knots_z * 3 * rows, width))
    reduced = halves(dot3((fity[0], fity[1]), forces))
    block = dot3(reduced, (fitx[0], fitx[1]))
    part[...] = block.reshape(part.shape)

    def pzcopy(side, dist):
        return pltpu.make_async_remote_copy(
            src_ref=part, dst_ref=part_z.at[1 - side, dist - 1],
            send_sem=pzs_sem.at[side, dist - 1], recv_sem=pzr_sem.at[1 - side, dist - 1],
            device_id=(slab - dist if side == 0 else slab + dist, strip), device_id_type=MESH,
        )

    def zfold(act_up, act_down):
        for dist in range(1, reach_z + 1):
            pl.when(slab < n_z - dist)(lambda: act_up(dist))
            pl.when(slab >= dist)(lambda: act_down(dist))

    zfold(lambda d: pzcopy(1, d).start(), lambda d: pzcopy(0, d).start())

    flat = (knots_y * pad_rows, ctl_pad)
    row_id = lax.broadcasted_iota(jnp.int32, flat, 0)
    inner_row = row_id % pad_rows
    knot_x = lax.broadcasted_iota(jnp.int32, flat, 1)
    used = (inner_row < knots_z * 3) & (knot_x < width // SPACING + 3)
    mass = (
        mass_of(slab * span_z + inner_row // 3, depth * n_z)
        * mass_of(strip * span_y + row_id // pad_rows, rows * n_y)
        * mass_of(knot_x, width)
    )
    weight = jnp.where(used, 1.0 / jnp.where(used, mass, 1.0), 0.0)

    zfold(lambda d: pzcopy(0, d).wait_recv(), lambda d: pzcopy(1, d).wait_recv())
    zfold(lambda d: pzcopy(1, d).wait_send(), lambda d: pzcopy(0, d).wait_send())
    for dist in range(1, reach_z + 1):
        offset = 3 * dist * span_z

        @pl.when(slab >= dist)
        def _():
            other = part_z[0, dist - 1].reshape(flat)
            moved = pltpu.roll(other, flat[0] - offset, 0)
            part[...] += jnp.where(inner_row < knots_z * 3 - offset, moved, 0.0).reshape(part.shape)

        @pl.when(slab < n_z - dist)
        def _():
            other = part_z[1, dist - 1].reshape(flat)
            moved = pltpu.roll(other, offset, 0)
            keep = (inner_row >= offset) & (inner_row < knots_z * 3)
            part[...] += jnp.where(keep, moved, 0.0).reshape(part.shape)

    def pycopy(side, dist):
        count = knots_y - dist * span_y
        start = 0 if side == 0 else dist * span_y
        return pltpu.make_async_remote_copy(
            src_ref=part.at[pl.ds(start, count)],
            dst_ref=part_y.at[1 - side, dist - 1, pl.ds(0, count)],
            send_sem=pys_sem.at[side, dist - 1], recv_sem=pyr_sem.at[1 - side, dist - 1],
            device_id=(slab, strip - dist if side == 0 else strip + dist), device_id_type=MESH,
        )

    def yfold(act_up, act_down):
        for dist in range(1, reach_y + 1):
            pl.when(strip < n_y - dist)(lambda: act_up(dist))
            pl.when(strip >= dist)(lambda: act_down(dist))

    yfold(lambda d: pycopy(1, d).start(), lambda d: pycopy(0, d).start())
    yfold(lambda d: pycopy(0, d).wait_recv(), lambda d: pycopy(1, d).wait_recv())
    yfold(lambda d: pycopy(1, d).wait_send(), lambda d: pycopy(0, d).wait_send())
    for dist in range(1, reach_y + 1):
        count = knots_y - dist * span_y

        @pl.when(strip >= dist)
        def _():
            part[0:count] += part_y[0, dist - 1, 0:count]

        @pl.when(strip < n_y - dist)
        def _():
            part[knots_y - count :] += part_y[1, dist - 1, 0:count]

    coef = part[...].reshape(flat) * weight
    lines = dot3(halves(coef), (evalx[0], evalx[1]))
    high, low = halves(lines)
    spread = jnp.concatenate([high, low, high], axis=0)
    power = jnp.sum(lines * dot(gram[...], spread))
    power_out[0] = jnp.full((8, LANE), power, jnp.float32)

    size = n_z * group

    def wcopy(step, stage):
        slot = step - 1 if stage == 0 else size - 1 + step - 1
        return pltpu.make_async_remote_copy(
            src_ref=power_out.at[stage], dst_ref=power_in.at[slot],
            send_sem=ws_sem.at[slot], recv_sem=wr_sem.at[slot],
            device_id=inner(step) if stage == 0 else outer(step), device_id_type=MESH,
        )

    for step in range(1, size):
        wcopy(step, 0).start()
    total = power_out[0]
    for step in range(1, size):
        wcopy(step, 0).wait_recv()
    for step in range(1, size):
        total = total + power_in[step - 1]
    power_out[1] = total
    for step in range(1, groups):
        wcopy(step, 1).start()
    for step in range(1, size):
        wcopy(step, 0).wait_send()
    zsends(lambda c: c.wait_send())
    to_sides(lambda c: c.wait_send(), ycopy)

    def sent(zside):
        def step(h, carry):
            to_sides(lambda c: c.wait_send(), lambda side: fcopy(side, zside, h))
            return carry

        lax.fori_loop(0, r, step, 0)

    pl.when(up)(lambda: sent(1))
    pl.when(down)(lambda: sent(0))

    for step in range(1, groups):
        wcopy(step, 1).wait_recv()
    for step in range(1, groups):
        total = total + power_in[size - 1 + step - 1]
    for step in range(1, groups):
        wcopy(step, 1).wait_send()
    entries = float(3 * depth * rows * width) * n_z * n_y
    scale = 1.0 / (jnp.sqrt(total / entries) + 1e-06)
    high, low = halves(lines * scale[0:1, 0:1])
    spread_ref[...] = jnp.concatenate([high, low, high], axis=0)


def field_kernel(table_ref, spread_ref, out_ref):
    out_ref[...] = dot(table_ref[...], spread_ref[...]).reshape(out_ref.shape)


def shards(n_z, n_y, fixed, moving):
    depth, rows, width = fixed.shape
    r = RADIUS
    eval_z = np_tables(depth)[0]
    eval_y, fit_y = np_tables(rows)
    eval_x, fit_x = np_tables(width)
    knots_z, knots_y, knots_x = eval_z.shape[1], eval_y.shape[1], eval_x.shape[1]
    lines = knots_z * 3
    pad_rows = -(-lines // 8) * 8
    ctl_pad = -(-knots_x // LANE) * LANE
    fitx = np.zeros((width, ctl_pad))
    fitx[:, :knots_x] = fit_x
    evalx = np.zeros((ctl_pad, width))
    evalx[:knots_x] = eval_x.T
    fity = np.zeros((knots_y, pad_rows, lines, rows))
    for line in range(lines):
        fity[:, line, line, :] = fit_y.T
    fity = fity.reshape(knots_y * pad_rows, lines * rows)
    evalzy = np.zeros((3, depth, rows, knots_y, pad_rows))
    for k in range(3):
        for a in range(knots_z):
            evalzy[k, :, :, :, a * 3 + k] = eval_z[:, a][:, None, None] * eval_y[None]
    evalzy = evalzy.reshape(3 * depth * rows, knots_y * pad_rows)
    gram = evalzy.T @ evalzy

    def thrice(table):
        high, low = np_halves(table)
        return jnp.asarray(np.concatenate([high, high, low], axis=1))

    def both(table):
        return jnp.asarray(np.stack(np_halves(table)))

    group = group_size(n_y)
    slots = n_z * group - 1 + n_y // group - 1
    reach_z = min((depth // SPACING + 2) // (depth // SPACING), n_z - 1)
    reach_y = min((rows // SPACING + 2) // (rows // SPACING), n_y - 1)
    dma = pltpu.SemaphoreType.DMA
    vmem = functools.partial(pltpu.VMEM, dtype=jnp.float32)
    half = functools.partial(pltpu.VMEM, dtype=jnp.bfloat16)
    lined = knots_y * pad_rows
    block = (knots_y, pad_rows, ctl_pad)
    anywhere = pl.BlockSpec(memory_space=pltpu.HBM)
    inside = pl.BlockSpec(memory_space=pltpu.VMEM)
    spread = pl.pallas_call(
        functools.partial(kernel, n_z, n_y, depth, rows, width, group, ctl_pad),
        out_shape=jax.ShapeDtypeStruct((3 * lined, width), jnp.bfloat16),
        in_specs=[anywhere] * 6,
        out_specs=inside,
        scratch_shapes=[
            vmem((2, depth + 2 * r, rows, width)),
            vmem((2, depth + 2 * r, 8, width)),
            vmem((2, depth + 2 * r, 8, width)),
            vmem((5, depth + 2 * r, rows, width)),
            vmem((depth + 2 * r, rows, width)),
            vmem((lines, rows, width)),
            half((2, width, ctl_pad)),
            half((2, ctl_pad, width)),
            half((2, lined, lines * rows)),
            half((lined, 3 * lined)),
            pltpu.SMEM((knots_z, depth), jnp.float32),
            vmem(block),
            vmem((2, reach_z) + block),
            vmem((2, reach_y) + block),
            vmem((2, 8, LANE)),
            vmem((slots, 8, LANE)),
            dma((2,)), dma((4,)),
            dma((2, r, 2)), dma((2, r, 2)),
            dma((2,)), dma((2,)),
            dma((2, 2, r)), dma((2, 2, r)),
            dma((2, reach_z)), dma((2, reach_z)),
            dma((2, reach_y)), dma((2, reach_y)),
            dma((slots,)), dma((slots,)),
        ],
        compiler_params=pltpu.CompilerParams(
            collective_id=0, has_side_effects=True, vmem_limit_bytes=60 * 1024 * 1024
        ),
        cost_estimate=pl.CostEstimate(flops=10**9, bytes_accessed=10**7, transcendentals=0),
    )(
        fixed, moving, both(fitx), both(evalx), both(fity), thrice(gram),
    )
    return pl.pallas_call(
        field_kernel,
        out_shape=jax.ShapeDtypeStruct((3, depth, rows, width), jnp.float32),
        grid=(3,),
        in_specs=[
            pl.BlockSpec((depth * rows, 3 * lined), lambda k: (k, 0)),
            pl.BlockSpec((3 * lined, width), lambda k: (0, 0)),
        ],
        out_specs=pl.BlockSpec((1, depth, rows, width), lambda k: (k, 0, 0, 0)),
        compiler_params=pltpu.CompilerParams(vmem_limit_bytes=32 * 1024 * 1024),
    )(thrice(evalzy), spread)


def solution(mesh):
    placed = (P("gz", "xy", None), P("gz", "xy", None))
    return jax.shard_map(
        functools.partial(shards, mesh.shape["gz"], mesh.shape["xy"]), mesh=mesh, in_specs=placed,
        out_specs=P(None, "gz", "xy", None), check_vma=False
    )
```

```python
import functools

import jax
import jax.numpy as jnp
import numpy as np
from jax import lax
from jax.experimental import pallas as pl
from jax.experimental.pallas import tpu as pltpu
from jax.sharding import PartitionSpec as P

RADIUS = 4
SPACING = 8
EPS = 1e-05
MESH = pl.DeviceIdType.MESH
LANE = 128


def np_basis(index, knot):
    span = index // SPACING
    t = (index - span * SPACING) / SPACING
    j = knot - span
    values = (
        (1 - t) ** 3 / 6,
        (3 * t**3 - 6 * t**2 + 4) / 6,
        (-3 * t**3 + 3 * t**2 + 3 * t + 1) / 6,
        t**3 / 6,
    )
    out = np.zeros(np.broadcast(index, knot).shape)
    for step in range(4):
        out = np.where(j == step, values[step], out)
    return out


def np_tables(extent):
    index = np.arange(extent)[:, None]
    value = np_basis(index, np.arange(extent // SPACING + 3)[None, :])
    return value, value**3 / (value**2).sum(axis=1, keepdims=True)


def energies():
    index = np.arange(SPACING)
    return [float((np_basis(index, np.full(SPACING, j)) ** 2).sum()) for j in range(4)]


def mass_of(knot, extent):
    total = jnp.zeros(knot.shape, jnp.float32)
    for j, energy in enumerate(energies()):
        start = knot - j
        total = total + jnp.where((start >= 0) & (start <= extent // SPACING - 1), energy, 0.0)
    return total


def group_size(count):
    size = 1
    while size * size < count and count % (size * 2) == 0:
        size *= 2
    return size


def dot(a, b):
    return jnp.dot(a, b, preferred_element_type=jnp.float32)


def halves(x):
    high = x.astype(jnp.bfloat16)
    return high, (x - high.astype(jnp.float32)).astype(jnp.bfloat16)


def np_halves(x):
    x = x.astype(np.float32)
    high = x.astype(jnp.bfloat16)
    return high, (x - high.astype(np.float32)).astype(jnp.bfloat16)


def dot3(a, b):
    return dot(a[0], b[0]) + (dot(a[1], b[0]) + dot(a[0], b[1]))


def kernel(
    n_z, n_y, depth, rows, width, group, ctl_pad,
    f_hbm, m_hbm, fitx_hbm, evalx_hbm, fity_hbm, evalzy_hbm, gram_hbm,
    field_ref, scale_ref,
    img, packout, packin, ysum, grady, acc, fitx, evalx, fity, evalzy, gram, fitz, part, part_z, part_y,
    power_out, power_in,
    own_sem, const_sem, zs_sem, zr_sem, ys_sem, yr_sem, fs_sem, fr_sem,
    pzs_sem, pzr_sem, pys_sem, pyr_sem, ws_sem, wr_sem,
):
    r = RADIUS
    slab, strip = lax.axis_index("gz"), lax.axis_index("xy")
    span_z, span_y = depth // SPACING, rows // SPACING
    knots_z, knots_y = span_z + 3, span_y + 3
    reach_z = min((span_z + 2) // span_z, n_z - 1)
    reach_y = min((span_y + 2) // span_y, n_y - 1)
    pad_rows = fity.shape[1] // knots_y
    up, down = slab < n_z - 1, slab > 0
    right, left = strip < n_y - 1, strip > 0
    after = rows + 2 * r

    own = [
        pltpu.make_async_copy(ref, img.at[i, pl.ds(r, depth)], own_sem.at[i])
        for i, ref in enumerate((f_hbm, m_hbm))
    ]
    consts = [
        pltpu.make_async_copy(src, dst, const_sem.at[i])
        for i, (src, dst) in enumerate(
            ((fitx_hbm, fitx), (evalx_hbm, evalx), (fity_hbm, fity), (evalzy_hbm, evalzy),
             (gram_hbm, gram))
        )
    ]
    for copy in own:
        copy.start()
    for copy in consts:
        copy.start()
    fit_table = np_tables(depth)[1]
    for a in range(knots_z):
        for z in range(depth):
            fitz[a, z] = jnp.float32(fit_table[z, a])

    barrier = pltpu.get_barrier_semaphore()
    lo_block = (strip // group) * group
    here = strip % group
    groups = n_y // group

    def beside(dist):
        if dist % group == 0:
            return []
        below = (strip >= dist) & (here < dist % group)
        above = (strip < n_y - dist) & (here >= group - dist % group)
        if dist > group:
            below, above = strip >= dist, strip < n_y - dist
        return [(below, strip - dist), (above, strip + dist)]

    def inner(step):
        place = (slab * group + here + step) % (n_z * group)
        return (place // group, lo_block + place % group)

    def outer(step):
        return (slab, (strip + step * group) % n_y)

    def greet(device):
        pl.semaphore_signal(barrier, inc=1, device_id=device, device_id_type=MESH)

    heard = n_z * group - 1 + groups - 1
    for step in range(1, n_z * group):
        greet(inner(step))
    for step in range(1, groups):
        greet(outer(step))
    for dist in range(1, reach_y + 1):
        for there, other in beside(dist):
            pl.when(there)(functools.partial(greet, (slab, other)))
            heard = heard + jnp.where(there, 1, 0)
    pl.semaphore_wait(barrier, heard)

    def zcopy(side, h, i):
        ref = (f_hbm, m_hbm)[i]
        src = h if side == 0 else depth - 1 - h
        dst = depth + r + h if side == 0 else r - 1 - h
        target = slab - 1 if side == 0 else slab + 1
        return pltpu.make_async_remote_copy(
            src_ref=ref.at[src], dst_ref=img.at[i, dst],
            send_sem=zs_sem.at[side, h, i], recv_sem=zr_sem.at[1 - side, h, i],
            device_id=(target, strip), device_id_type=MESH,
        )

    def zsends(act):
        for h in range(r):
            for i in range(2):
                pl.when(up)(lambda: act(zcopy(1, h, i)))
                pl.when(down)(lambda: act(zcopy(0, h, i)))

    zsends(lambda c: c.start())

    def zwait(side, h):
        plane = jnp.where(side == 0, r - 1 - h, depth + r + h)
        for i in range(2):
            pltpu.make_async_remote_copy(
                src_ref=img.at[i, plane], dst_ref=img.at[i, plane],
                send_sem=zs_sem.at[side, h, i], recv_sem=zr_sem.at[side, h, i],
                device_id=(slab, strip), device_id_type=MESH,
            ).wait_recv()

    def pack(plane):
        first = lax.broadcasted_iota(jnp.int32, (8, width), 0) < 4
        f0, m0 = img[0, plane, 0:8, :], img[1, plane, 0:8, :]
        f1, m1 = img[0, plane, rows - 8 : rows, :], img[1, plane, rows - 8 : rows, :]
        packout[0, plane] = jnp.where(first, m0, pltpu.roll(f0, 4, 0))
        packout[1, plane] = jnp.where(first, pltpu.roll(f1, 4, 0), m1)

    def ycopy(side):
        return pltpu.make_async_remote_copy(
            src_ref=packout.at[side, pl.ds(r, depth)], dst_ref=packin.at[1 - side, pl.ds(r, depth)],
            send_sem=ys_sem.at[side], recv_sem=yr_sem.at[1 - side],
            device_id=(slab, strip - 1 if side == 0 else strip + 1), device_id_type=MESH,
        )

    def fcopy(side, zside, h):
        plane = jnp.where(zside == 0, r - 1 - h, depth + r + h)
        return pltpu.make_async_remote_copy(
            src_ref=packout.at[side, plane], dst_ref=packin.at[1 - side, plane],
            send_sem=fs_sem.at[side, zside, h], recv_sem=fr_sem.at[1 - side, zside, h],
            device_id=(slab, strip - 1 if side == 0 else strip + 1), device_id_type=MESH,
        )

    def to_sides(act, make):
        pl.when(left)(lambda: act(make(0)))
        pl.when(right)(lambda: act(make(1)))

    def from_sides(make):
        pl.when(left)(lambda: make(1).wait_recv())
        pl.when(right)(lambda: make(0).wait_recv())

    for copy in own:
        copy.wait()

    def pack_own(p, carry):
        pack(p + r)
        return carry

    lax.fori_loop(0, depth, pack_own, 0)
    to_sides(lambda c: c.start(), ycopy)

    @pl.when(jnp.logical_not(left))
    def _():
        packin[0] = jnp.zeros_like(packin[0])

    @pl.when(jnp.logical_not(right))
    def _():
        packin[1] = jnp.zeros_like(packin[1])

    @pl.when(jnp.logical_not(down))
    def _():
        img[:, 0:r] = jnp.zeros((2, r, rows, width), jnp.float32)
        ysum[:, 0:r] = jnp.zeros((5, r, rows, width), jnp.float32)

    @pl.when(jnp.logical_not(up))
    def _():
        img[:, depth + r :] = jnp.zeros((2, r, rows, width), jnp.float32)
        ysum[:, depth + r :] = jnp.zeros((5, r, rows, width), jnp.float32)

    acc[...] = jnp.zeros_like(acc)

    chunk = 2 * LANE

    def rows_of(plane):
        first = lax.broadcasted_iota(jnp.int32, (8, chunk), 0) < 4
        filler = jnp.zeros((8, chunk), jnp.float32)
        for x in range(0, width, chunk):
            cols = slice(x, x + chunk)
            lo, hi = packin[0, plane, :, cols], packin[1, plane, :, cols]

            def around(i, low, high):
                t = pltpu.roll(jnp.concatenate([img[i, plane, :, cols], filler], axis=0), 4, 0)
                return jnp.concatenate(
                    [jnp.where(first, low, t[0:8]), t[8 : after - 8],
                     jnp.where(first, t[after - 8 :], high)], axis=0)

            f = around(0, lo, hi)
            m = around(1, pltpu.roll(lo, 4, 0), pltpu.roll(hi, 4, 0))
            for q, v in enumerate((f, m, f * f, m * m, f * m)):
                s = v + pltpu.roll(v, after - 1, 0)
                s = s + pltpu.roll(s, after - 2, 0)
                s = s + pltpu.roll(s, after - 4, 0)
                ysum[q, plane, :, cols] = s[0:rows] + v[8:after]
            diff = pltpu.roll(m, after - 5, 0) - pltpu.roll(m, after - 3, 0)
            grady[plane, :, cols] = diff[0:rows] * 0.5

    inv = 1.0 / float((2 * r + 1) ** 3)
    wide = width + LANE
    tail = jnp.zeros((8, LANE), jnp.float32)

    def force_of(z):
        for t in range(0, rows, 8):
            tile = slice(t, t + 8)
            sums = []
            for q in range(5):
                total = ysum[q, z, tile, :]
                for k in range(1, 2 * r + 1):
                    total = total + ysum[q, z + k, tile, :]
                total = jnp.concatenate([total, tail], axis=1)
                total = total + pltpu.roll(total, 1, 1) + pltpu.roll(total, wide - 1, 1)
                total = total + pltpu.roll(total, 3, 1) + pltpu.roll(total, wide - 3, 1)
                sums.append(total[:, 0:width] * inv)
            mean_f, mean_m, ff, mm, fm = sums
            cov = fm - mean_f * mean_m
            var_f = ff - mean_f * mean_f
            var_m = mm - mean_m * mean_m
            f, m = img[0, z + r, tile, :], img[1, z + r, tile, :]
            factor = 2.0 * cov / (var_f * var_m + EPS)
            resid = f - mean_f - cov / (var_m + EPS) * (m - mean_m)
            common = factor * resid
            mw = jnp.concatenate([m, tail], axis=1)
            gx = (pltpu.roll(mw, wide - 1, 1) - pltpu.roll(mw, 1, 1))[:, 0:width] * 0.5
            gz = (img[1, z + r + 1, tile, :] - img[1, z + r - 1, tile, :]) * 0.5
            gy = grady[z + r, tile, :]
            for k, g in enumerate((gz, gy, gx)):
                v = common * g
                for a in range(knots_z):
                    acc[a * 3 + k, tile, :] += v * fitz[a, z]

    from_sides(ycopy)

    def own_rows(p, carry):
        rows_of(p + r)
        return carry

    lax.fori_loop(0, depth, own_rows, 0)

    @pl.when(jnp.logical_and(up, down))
    def _():
        def step(h, carry):
            zwait(0, h)
            pack(r - 1 - h)
            to_sides(lambda c: c.start(), lambda side: fcopy(side, 0, h))
            from_sides(lambda side: fcopy(side, 0, h))
            rows_of(r - 1 - h)
            return carry

        lax.fori_loop(0, r, step, 0)

    main = jnp.where(up, 1, 0)

    def place(s):
        return jnp.where(up, s, depth - 1 - s)

    def early(s, carry):
        force_of(place(s))
        return carry

    lax.fori_loop(0, (depth - r) // 2, early, 0)

    def pass_on(h, carry):
        zwait(main, h)
        pack(jnp.where(up, depth + r + h, r - 1 - h))
        to_sides(lambda c: c.start(), lambda side: fcopy(side, main, h))
        return carry

    lax.fori_loop(0, r, pass_on, 0)
    lax.fori_loop((depth - r) // 2, depth - r, early, 0)

    def late(h, carry):
        from_sides(lambda side: fcopy(side, main, h))
        rows_of(jnp.where(up, depth + r + h, r - 1 - h))
        force_of(place(depth - r + h))
        return carry

    lax.fori_loop(0, r, late, 0)

    for copy in consts:
        copy.wait()
    forces = halves(acc[...].reshape(knots_z * 3 * rows, width))
    reduced = halves(dot3((fity[0], fity[1]), forces))
    block = dot3(reduced, (fitx[0], fitx[1]))
    part[...] = block.reshape(part.shape)

    def pzcopy(side, dist):
        return pltpu.make_async_remote_copy(
            src_ref=part, dst_ref=part_z.at[1 - side, dist - 1],
            send_sem=pzs_sem.at[side, dist - 1], recv_sem=pzr_sem.at[1 - side, dist - 1],
            device_id=(slab - dist if side == 0 else slab + dist, strip), device_id_type=MESH,
        )

    def zfold(act_up, act_down):
        for dist in range(1, reach_z + 1):
            pl.when(slab < n_z - dist)(lambda: act_up(dist))
            pl.when(slab >= dist)(lambda: act_down(dist))

    zfold(lambda d: pzcopy(1, d).start(), lambda d: pzcopy(0, d).start())

    flat = (knots_y * pad_rows, ctl_pad)
    row_id = lax.broadcasted_iota(jnp.int32, flat, 0)
    inner_row = row_id % pad_rows
    knot_x = lax.broadcasted_iota(jnp.int32, flat, 1)
    used = (inner_row < knots_z * 3) & (knot_x < width // SPACING + 3)
    mass = (
        mass_of(slab * span_z + inner_row // 3, depth * n_z)
        * mass_of(strip * span_y + row_id // pad_rows, rows * n_y)
        * mass_of(knot_x, width)
    )
    weight = jnp.where(used, 1.0 / jnp.where(used, mass, 1.0), 0.0)

    zfold(lambda d: pzcopy(0, d).wait_recv(), lambda d: pzcopy(1, d).wait_recv())
    zfold(lambda d: pzcopy(1, d).wait_send(), lambda d: pzcopy(0, d).wait_send())
    for dist in range(1, reach_z + 1):
        offset = 3 * dist * span_z

        @pl.when(slab >= dist)
        def _():
            other = part_z[0, dist - 1].reshape(flat)
            moved = pltpu.roll(other, flat[0] - offset, 0)
            part[...] += jnp.where(inner_row < knots_z * 3 - offset, moved, 0.0).reshape(part.shape)

        @pl.when(slab < n_z - dist)
        def _():
            other = part_z[1, dist - 1].reshape(flat)
            moved = pltpu.roll(other, offset, 0)
            keep = (inner_row >= offset) & (inner_row < knots_z * 3)
            part[...] += jnp.where(keep, moved, 0.0).reshape(part.shape)

    def pycopy(side, dist):
        count = knots_y - dist * span_y
        start = 0 if side == 0 else dist * span_y
        return pltpu.make_async_remote_copy(
            src_ref=part.at[pl.ds(start, count)],
            dst_ref=part_y.at[1 - side, dist - 1, pl.ds(0, count)],
            send_sem=pys_sem.at[side, dist - 1], recv_sem=pyr_sem.at[1 - side, dist - 1],
            device_id=(slab, strip - dist if side == 0 else strip + dist), device_id_type=MESH,
        )

    def yfold(act_up, act_down):
        for dist in range(1, reach_y + 1):
            pl.when(strip < n_y - dist)(lambda: act_up(dist))
            pl.when(strip >= dist)(lambda: act_down(dist))

    yfold(lambda d: pycopy(1, d).start(), lambda d: pycopy(0, d).start())
    yfold(lambda d: pycopy(0, d).wait_recv(), lambda d: pycopy(1, d).wait_recv())
    yfold(lambda d: pycopy(1, d).wait_send(), lambda d: pycopy(0, d).wait_send())
    for dist in range(1, reach_y + 1):
        count = knots_y - dist * span_y

        @pl.when(strip >= dist)
        def _():
            part[0:count] += part_y[0, dist - 1, 0:count]

        @pl.when(strip < n_y - dist)
        def _():
            part[knots_y - count :] += part_y[1, dist - 1, 0:count]

    coef = part[...].reshape(flat) * weight
    lines = dot3(halves(coef), (evalx[0], evalx[1]))
    high, low = halves(lines)
    spread = jnp.concatenate([high, low, high], axis=0)
    power = jnp.sum(lines * dot(gram[...], spread))
    power_out[0] = jnp.full((8, LANE), power, jnp.float32)

    size = n_z * group

    def wcopy(step, stage):
        slot = step - 1 if stage == 0 else size - 1 + step - 1
        return pltpu.make_async_remote_copy(
            src_ref=power_out.at[stage], dst_ref=power_in.at[slot],
            send_sem=ws_sem.at[slot], recv_sem=wr_sem.at[slot],
            device_id=inner(step) if stage == 0 else outer(step), device_id_type=MESH,
        )

    for step in range(1, size):
        wcopy(step, 0).start()
    voxels = depth * rows
    for k in range(3):
        field_ref[k] = dot(evalzy[k * voxels : (k + 1) * voxels, :], spread).reshape(
            depth, rows, width)
    total = power_out[0]
    for step in range(1, size):
        wcopy(step, 0).wait_recv()
    for step in range(1, size):
        total = total + power_in[step - 1]
    power_out[1] = total
    for step in range(1, groups):
        wcopy(step, 1).start()
    for step in range(1, size):
        wcopy(step, 0).wait_send()
    zsends(lambda c: c.wait_send())
    to_sides(lambda c: c.wait_send(), ycopy)

    def sent(zside):
        def step(h, carry):
            to_sides(lambda c: c.wait_send(), lambda side: fcopy(side, zside, h))
            return carry

        lax.fori_loop(0, r, step, 0)

    pl.when(up)(lambda: sent(1))
    pl.when(down)(lambda: sent(0))

    for step in range(1, groups):
        wcopy(step, 1).wait_recv()
    for step in range(1, groups):
        total = total + power_in[size - 1 + step - 1]
    for step in range(1, groups):
        wcopy(step, 1).wait_send()
    entries = float(3 * depth * rows * width) * n_z * n_y
    scale = 1.0 / (jnp.sqrt(total / entries) + 1e-06)
    scale_ref[...] = jnp.broadcast_to(scale[0:1, 0:1], (rows, width))


def shards(n_z, n_y, fixed, moving):
    depth, rows, width = fixed.shape
    r = RADIUS
    eval_z = np_tables(depth)[0]
    eval_y, fit_y = np_tables(rows)
    eval_x, fit_x = np_tables(width)
    knots_z, knots_y, knots_x = eval_z.shape[1], eval_y.shape[1], eval_x.shape[1]
    lines = knots_z * 3
    pad_rows = -(-lines // 8) * 8
    ctl_pad = -(-knots_x // LANE) * LANE
    fitx = np.zeros((width, ctl_pad))
    fitx[:, :knots_x] = fit_x
    evalx = np.zeros((ctl_pad, width))
    evalx[:knots_x] = eval_x.T
    fity = np.zeros((knots_y, pad_rows, lines, rows))
    for line in range(lines):
        fity[:, line, line, :] = fit_y.T
    fity = fity.reshape(knots_y * pad_rows, lines * rows)
    evalzy = np.zeros((3, depth, rows, knots_y, pad_rows))
    for k in range(3):
        for a in range(knots_z):
            evalzy[k, :, :, :, a * 3 + k] = eval_z[:, a][:, None, None] * eval_y[None]
    evalzy = evalzy.reshape(3 * depth * rows, knots_y * pad_rows)
    gram = evalzy.T @ evalzy

    def thrice(table):
        high, low = np_halves(table)
        return jnp.asarray(np.concatenate([high, high, low], axis=1))

    def both(table):
        return jnp.asarray(np.stack(np_halves(table)))

    group = group_size(n_y)
    slots = n_z * group - 1 + n_y // group - 1
    reach_z = min((depth // SPACING + 2) // (depth // SPACING), n_z - 1)
    reach_y = min((rows // SPACING + 2) // (rows // SPACING), n_y - 1)
    dma = pltpu.SemaphoreType.DMA
    vmem = functools.partial(pltpu.VMEM, dtype=jnp.float32)
    half = functools.partial(pltpu.VMEM, dtype=jnp.bfloat16)
    lined = knots_y * pad_rows
    block = (knots_y, pad_rows, ctl_pad)
    anywhere = pl.BlockSpec(memory_space=pltpu.HBM)
    inside = pl.BlockSpec(memory_space=pltpu.VMEM)
    field, scale = pl.pallas_call(
        functools.partial(kernel, n_z, n_y, depth, rows, width, group, ctl_pad),
        out_shape=(
            jax.ShapeDtypeStruct((3, depth, rows, width), jnp.float32),
            jax.ShapeDtypeStruct((rows, width), jnp.float32),
        ),
        in_specs=[anywhere] * 7,
        out_specs=(inside, inside),
        scratch_shapes=[
            vmem((2, depth + 2 * r, rows, width)),
            vmem((2, depth + 2 * r, 8, width)),
            vmem((2, depth + 2 * r, 8, width)),
            vmem((5, depth + 2 * r, rows, width)),
            vmem((depth + 2 * r, rows, width)),
            vmem((lines, rows, width)),
            half((2, width, ctl_pad)),
            half((2, ctl_pad, width)),
            half((2, lined, lines * rows)),
            half((3 * depth * rows, 3 * lined)),
            half((lined, 3 * lined)),
            pltpu.SMEM((knots_z, depth), jnp.float32),
            vmem(block),
            vmem((2, reach_z) + block),
            vmem((2, reach_y) + block),
            vmem((2, 8, LANE)),
            vmem((slots, 8, LANE)),
            dma((2,)), dma((5,)),
            dma((2, r, 2)), dma((2, r, 2)),
            dma((2,)), dma((2,)),
            dma((2, 2, r)), dma((2, 2, r)),
            dma((2, reach_z)), dma((2, reach_z)),
            dma((2, reach_y)), dma((2, reach_y)),
            dma((slots,)), dma((slots,)),
        ],
        compiler_params=pltpu.CompilerParams(
            collective_id=0, has_side_effects=True, vmem_limit_bytes=60 * 1024 * 1024
        ),
        cost_estimate=pl.CostEstimate(flops=10**9, bytes_accessed=10**7, transcendentals=0),
    )(
        fixed, moving, both(fitx), both(evalx), both(fity), thrice(evalzy), thrice(gram),
    )
    return field * scale[None, None]


def solution(mesh):
    placed = (P("gz", "xy", None), P("gz", "xy", None))
    return jax.shard_map(
        functools.partial(shards, mesh.shape["gz"], mesh.shape["xy"]), mesh=mesh, in_specs=placed,
        out_specs=P(None, "gz", "xy", None), check_vma=False
    )
```
